128 devices in a mesh: ax: 8 (over x, core), az: 16 (over z, y).
Axes of the slice: x: 4, y: 4, z: 4, core: 2. Of those that a mesh axis runs over, the one named last changes fastest.
Arguments:
- state: float32 [4, 2, 16, 1024, 2048], P(None, None, None, 'az', 'ax'), as said below
- inflow: float32 [4, 2, 16, 1024], P(None, None, None, 'az'), as said below
- courant: float32 [16, 2048], P(None, 'ax'), may hold values from 1 to 12288
- mode_number: int32 [1024], P('az'), may hold values from 0 to 1023, as said below
- partner_table: int32 [1024], P('az'), may hold values from 0 to 1023, as said below
Outputs:
- new_state: float32 [4, 2, 16, 1024, 2048], P(None, None, None, 'az', 'ax')
The draws below stay inside these ranges and needn't reach their ends.
Inputs may be any that keep to these rules, and one draw needn't show every extreme that they name: `mode_number`: a permutation of 0 .. 1023; where slot s < 512 holds k, slot s + 512 holds (1024 - k) mod 1024, except for one pair of slots s0 and s0 + 512 that hold 0 and 512. partner_table[s] = s at the two slots holding modes 0 and 512, and (s + 512) mod 1024 at all others. `state`: conjugate-symmetric over the slots: slot (s + 512) mod 1024 holds the complex conjugate of slot s, except at the two slots holding modes 0 and 512, whose imaginary parts are zero. `inflow`: conjugate-symmetric over the slots as state.
All inputs are finite; a program needn't handle non-finite values.
Results may differ from the reference program's by a relative error of at most 0.00012.
Values sent between devices are 32-bit elements; how exact they have to be, the bound alone decides.
A program may use at most 320 MiB of HBM per device.

```python
import math
import jax
import jax.numpy as jnp
from jax import lax

M = 1024
FIELDS = 4
RADIAL_POINTS = 16
AXIAL_CELLS = 2048


def mode_layout(key):
    half_modes = M // 2
    key_perm, key_flip = jax.random.split(key)
    picked = jax.random.permutation(key_perm, half_modes).astype(jnp.int32)
    mirror_flag = jax.random.randint(key_flip, (half_modes,), 0, 2)
    first_half = jnp.where(mirror_flag == 1, (M - picked) % M, picked)
    second_half = jnp.where(picked == 0, half_modes, (M - first_half) % M)
    mode_ids = jnp.concatenate([first_half, second_half]).astype(jnp.int32)
    slot_ids = jnp.arange(half_modes, dtype=jnp.int32)
    self_first = picked == 0
    partner_ids = jnp.concatenate([jnp.where(self_first, slot_ids, slot_ids + half_modes), jnp.where(self_first, slot_ids + half_modes, slot_ids)]).astype(jnp.int32)
    return (mode_ids, partner_ids, self_first)


def mirror_modes(real_first, imag_first, real_extra, self_first, mode_axis):
    mask_shape = [1] * real_first.ndim
    mask_shape[mode_axis] = self_first.shape[0]
    self_mask = self_first.reshape(mask_shape)
    imag_clean = jnp.where(self_mask, 0.0, imag_first)
    real_second = jnp.where(self_mask, real_extra, real_first)
    real_all = jnp.concatenate([real_first, real_second], axis=mode_axis)
    imag_all = jnp.concatenate([imag_clean, -imag_clean], axis=mode_axis)
    return jnp.stack([real_all, imag_all], axis=1)


def draw_mode_number(key, part):
    mode_ids, partner_ids, self_first = mode_layout(key)
    return mode_ids


def draw_partner_table(key, part):
    mode_ids, partner_ids, self_first = mode_layout(key)
    return partner_ids


def draw_state(key, part):
    mode_ids, partner_ids, self_first = mode_layout(key)
    key = jax.random.fold_in(key, 3)
    key_real, key_imag, key_extra = jax.random.split(key, 3)
    half_modes = M // 2
    full_shape = (FIELDS, RADIAL_POINTS, half_modes, AXIAL_CELLS)
    extra_shape = (FIELDS, RADIAL_POINTS, 1, AXIAL_CELLS)
    real_first = jax.random.normal(key_real, full_shape, jnp.float32)
    imag_first = jax.random.normal(key_imag, full_shape, jnp.float32)
    real_extra = jax.random.normal(key_extra, extra_shape, jnp.float32)
    return mirror_modes(real_first, imag_first, real_extra, self_first, 2)


def draw_inflow(key, part):
    mode_ids, partner_ids, self_first = mode_layout(key)
    key = jax.random.fold_in(key, 5)
    key_real, key_imag, key_extra = jax.random.split(key, 3)
    half_modes = M // 2
    full_shape = (FIELDS, RADIAL_POINTS, half_modes)
    extra_shape = (FIELDS, RADIAL_POINTS, 1)
    real_first = jax.random.normal(key_real, full_shape, jnp.float32)
    imag_first = jax.random.normal(key_imag, full_shape, jnp.float32)
    real_extra = jax.random.normal(key_extra, extra_shape, jnp.float32)
    return mirror_modes(real_first, imag_first, real_extra, self_first, 2)


def draw_courant(key, part):
    key = jax.random.fold_in(key, 7)
    key_select, key_noise, key_spike, key_background = jax.random.split(key, 4)
    picked = jax.random.uniform(key_select, (RADIAL_POINTS, 1), jnp.float32)
    slow_line = picked < 0.5
    rough = jnp.exp(jax.random.uniform(key_noise, (RADIAL_POINTS, AXIAL_CELLS), jnp.float32, -0.6931, 0.6931))
    background_value = jnp.where(slow_line, 3.0 * AXIAL_CELLS * rough, 40.0 * rough)
    spike_cell_rows = jax.random.randint(key_spike, (2,), 0, AXIAL_CELLS)
    cell_index = jnp.arange(AXIAL_CELLS, dtype=jnp.int32)
    spike_mask = jnp.any(cell_index[None, :] == spike_cell_rows[:, None], axis=0)
    spike_value = jax.random.uniform(key_background, (RADIAL_POINTS, AXIAL_CELLS), jnp.float32, 1.0, 4.0)
    return jnp.where(spike_mask[None, :], spike_value, background_value)


def setup_inputs(seed: int = 0) -> dict:
    seeds = jax.random.split(jax.random.key(seed), 6)
    state = draw_state(jax.random.fold_in(seeds[5], 71), 0)
    inflow = draw_inflow(jax.random.fold_in(seeds[5], 71), 0)
    courant = draw_courant(jax.random.fold_in(seeds[5], 71), 0)
    mode_number = draw_mode_number(jax.random.fold_in(seeds[5], 71), 0)
    partner_table = draw_partner_table(jax.random.fold_in(seeds[5], 71), 0)
    return {"state": state, "inflow": inflow, "courant": courant, "mode_number": mode_number, "partner_table": partner_table}


section_factor = 0.5
viscosity = 0.02

def contract(pattern, operand_a, operand_b):
    return jnp.einsum(pattern, operand_a, operand_b, precision=lax.Precision.HIGHEST)

def dft_tables(mode_ids, point_count):
    angles = jnp.arange(point_count, dtype=jnp.int32)
    phase_ids = mode_ids[:, None] * angles[None, :] % point_count
    angle_values = phase_ids.astype(jnp.float32) * (2.0 * math.pi / point_count)
    norm_factor = 1.0 / math.sqrt(point_count)
    return (jnp.cos(angle_values) * norm_factor, jnp.sin(angle_values) * norm_factor)

def signed_modes(mode_ids, point_count):
    half_count = point_count // 2
    shifted = jnp.where(mode_ids == half_count, 0, mode_ids - point_count)
    return jnp.where(mode_ids < half_count, mode_ids, shifted).astype(jnp.float32)

def radii(radial_ids, radial_count, point_count):
    return point_count / (2.0 * math.pi) * (0.6 + 0.4 * (radial_ids.astype(jnp.float32) + 0.5) / radial_count)

def reference(state, inflow, courant, mode_number, partner_table):
    point_count = state.shape[3]
    radial_count = state.shape[2]
    cos_table, sin_table = dft_tables(mode_number, point_count)
    wavenumber = signed_modes(mode_number, point_count)
    radial_inverse = 1.0 / radii(jnp.arange(radial_count, dtype=jnp.int32), radial_count, point_count)

    def per_radius(carried):
        radial_slab, inverse_here = carried
        real_parts = jnp.stack([radial_slab[0, 0] - radial_slab[1, 1], radial_slab[2, 0] - radial_slab[3, 1]])
        imag_parts = jnp.stack([radial_slab[0, 1] + radial_slab[1, 0], radial_slab[2, 1] + radial_slab[3, 0]])
        field_real = contract('psx,sj->pjx', real_parts, cos_table) - contract('psx,sj->pjx', imag_parts, sin_table)
        field_imag = contract('psx,sj->pjx', real_parts, sin_table) + contract('psx,sj->pjx', imag_parts, cos_table)
        fields = jnp.stack([field_real[0], field_imag[0], field_real[1], field_imag[1]])
        axial_flux = fields[0][None] * fields
        azim_flux = fields[2][None] * fields * inverse_here
        padded = jnp.pad(axial_flux, ((0, 0), (0, 0), (1, 1)))
        divergence = -(padded[:, :, 2:] - padded[:, :, :-2]) * 0.5
        spec_real = contract('cjx,sj->csx', divergence, cos_table) + contract('cjx,sj->csx', azim_flux, sin_table)
        spec_imag = contract('cjx,sj->csx', azim_flux, cos_table) - contract('cjx,sj->csx', divergence, sin_table)
        mate_real = jnp.take(spec_real, partner_table, axis=1)
        mate_imag = jnp.take(spec_imag, partner_table, axis=1)
        wave_ratio = (wavenumber * inverse_here)[None, :, None]
        real_terms = 0.5 * (spec_real + mate_real) - 0.5 * wave_ratio * (spec_real - mate_real)
        imag_terms = 0.5 * (spec_imag - mate_imag) - 0.5 * wave_ratio * (spec_imag + mate_imag)
        return jnp.stack([real_terms, imag_terms], axis=1)
    explicit_terms = lax.map(per_radius, (jnp.moveaxis(state, 2, 0), radial_inverse))
    explicit_terms = jnp.moveaxis(explicit_terms, 0, 2)
    ratio_all = wavenumber[None, :] * radial_inverse[:, None]
    damping = viscosity * ratio_all * ratio_all
    section_input = state + section_factor * (explicit_terms - damping[None, None, :, :, None] * state)
    weight = courant / (1.0 + courant)

    def advance(previous, column):
        section_column, weight_column = column
        weight_bcast = weight_column[None, None, :, None]
        current = weight_bcast * previous + (1.0 - weight_bcast) * section_column
        return (current, current)
    final_value, swept_cells = lax.scan(advance, inflow, (jnp.moveaxis(section_input, 4, 0), jnp.moveaxis(weight, 1, 0)))
    return jnp.moveaxis(swept_cells, 0, 4)
```

```python
import functools
import math

import jax
import jax.numpy as jnp
from jax import lax
from jax.experimental import pallas as pl
from jax.experimental.pallas import tpu as pltpu
from jax.sharding import PartitionSpec as P

section_factor = 0.5
viscosity = 0.02
M = 1024
HALF = M // 2
FIELDS = 4
NR = 16
SLOTS = 64
CELLS = 256
NAZ = 16
NAX = 8
LANES = 128
MESH = pl.DeviceIdType.MESH
F32 = jnp.float32
BF16 = jnp.bfloat16


def split(value):
    high = value.astype(BF16)
    low = (value - high.astype(F32)).astype(BF16)
    return high, low


def inverse_radius(radial_id):
    ratio = (0.6 + 0.4 * (radial_id.astype(F32) + 0.5) / NR) * (M / (2.0 * math.pi))
    return 1.0 / ratio


def cos_sin(phase):
    quadrant = lax.shift_right_logical(phase + 128, 8)
    angle = (phase - quadrant * 256).astype(F32) * (2.0 * math.pi / M)
    square = angle * angle
    sine = angle * (
        1.0
        + square
        * (-1.0 / 6 + square * (1.0 / 120 + square * (-1.0 / 5040 + square * (1.0 / 362880))))
    )
    cosine = 1.0 + square * (
        -0.5 + square * (1.0 / 24 + square * (-1.0 / 720 + square * (1.0 / 40320)))
    )
    odd = (quadrant & 1) == 1
    norm = 1.0 / math.sqrt(M)
    cos_value = jnp.where(odd, sine, cosine)
    sin_value = jnp.where(odd, cosine, sine)
    cos_sign = jnp.where(((quadrant + 1) & 2) == 2, -norm, norm)
    sin_sign = jnp.where((quadrant & 2) == 2, -norm, norm)
    return cos_value * cos_sign, sin_value * sin_sign


def signed(modes):
    return jnp.where(modes < HALF, modes, jnp.where(modes == HALF, 0.0, modes - M))


def is_self(modes):
    return jnp.where((modes == 0.0) | (modes == float(HALF)), 1.0, 0.0)


def fold_rows(value):
    rows, lanes = value.shape
    return jnp.sum(value.reshape(rows // 8, 8, lanes), axis=0)


def kernel(
    state_ref, courant_ref, mode_ref, inflow_ref,
    acc_ref, incoming_ref, reach_ref,
    st, send_buf, x_buf, mode_buf, mode_sub, own_sub,
    cos_f, sin_f, cos_r, sin_r, rhs_a, rhs_b, tcat,
    fp, fm, fmid, d_mid, halo_send, halo_recv,
    lc_ref, lc_t, om_t, e_raw, e_send, e_recv, lhs_cat, rel_buf,
    st_sem, f_send, f_recv, m_send, m_recv, own_x, h_send, h_recv,
    e_send_sem, e_recv_sem, own_e, out_sem, rel_send, rel_recv,
):
    ax = lax.axis_index("ax")
    az = lax.axis_index("az")
    z = lax.div(az, 4)
    y = lax.rem(az, 4)

    def az_target(offset):
        return lax.rem(z + lax.div(offset, 4), 4) * 4 + lax.rem(y + lax.rem(offset, 4), 4)

    def ax_target(offset):
        return lax.rem(ax + offset, NAX)

    def start_state(offset, carry):
        target = az_target(offset)
        pltpu.make_async_copy(
            state_ref.at[:, :, target], st.at[target], st_sem.at[target]
        ).start()
        return carry

    lax.fori_loop(0, NAZ, start_state, 0)

    barrier = pltpu.get_barrier_semaphore()

    def greet_az(offset, carry):
        pl.semaphore_signal(barrier, inc=1, device_id=(ax, az_target(offset)), device_id_type=MESH)
        return carry

    def greet_ax(offset, carry):
        pl.semaphore_signal(barrier, inc=1, device_id=(ax_target(offset), az), device_id_type=MESH)
        return carry

    lax.fori_loop(1, NAZ, greet_az, 0)
    lax.fori_loop(1, NAX, greet_ax, 0)

    mode_buf[az] = mode_ref[...]
    pl.semaphore_wait(barrier, NAZ - 1 + NAX - 1)

    def send_modes(offset, carry):
        pltpu.make_async_remote_copy(
            src_ref=mode_ref, dst_ref=mode_buf.at[az], send_sem=m_send, recv_sem=m_recv,
            device_id=(ax, az_target(offset)), device_id_type=MESH,
        ).start()
        return carry

    lax.fori_loop(1, NAZ, send_modes, 0)

    def send_piece(target, chunk, pair):
        comps = pl.ds(pair * 2, 2)
        pltpu.make_async_remote_copy(
            src_ref=send_buf.at[target, chunk, comps],
            dst_ref=x_buf.at[chunk, comps, pl.ds(az * SLOTS, SLOTS), :],
            send_sem=f_send, recv_sem=f_recv.at[chunk],
            device_id=(ax, target), device_id_type=MESH,
        ).start()

    def pack(offset, carry):
        target = az_target(offset)
        pltpu.make_async_copy(
            state_ref.at[:, :, target], st.at[target], st_sem.at[target]
        ).wait()
        for pair in range(2):
            for chunk in range(2):
                cells = pl.ds(chunk * LANES, LANES)
                send_buf[target, chunk, 2 * pair] = (
                    st[target, 2 * pair, 0, :, cells] - st[target, 2 * pair + 1, 1, :, cells]
                )
                send_buf[target, chunk, 2 * pair + 1] = (
                    st[target, 2 * pair, 1, :, cells] + st[target, 2 * pair + 1, 0, :, cells]
                )

        @pl.when(offset > 0)
        def _():
            send_piece(target, 0, 0)

        return carry

    lax.fori_loop(0, NAZ, pack, 0)
    for chunk, pair in ((0, 1), (1, 0), (1, 1)):

        def send_more(offset, carry, chunk=chunk, pair=pair):
            send_piece(az_target(offset), chunk, pair)
            return carry

        lax.fori_loop(1, NAZ, send_more, 0)

    def own_copy(chunk):
        return pltpu.make_async_copy(
            send_buf.at[az, chunk],
            x_buf.at[chunk, :, pl.ds(az * SLOTS, SLOTS), :],
            own_x.at[chunk],
        )

    own_copy(0).start()
    own_copy(1).start()

    courant = courant_ref[...]
    log_weight = -jnp.log(1.0 + 1.0 / courant)
    row_ids = lax.broadcasted_iota(jnp.int32, (CELLS, CELLS), 0)
    col_ids = lax.broadcasted_iota(jnp.int32, (CELLS, CELLS), 1)
    upper = jnp.where(row_ids <= col_ids, 1.0, 0.0)
    log_cum = jnp.dot(
        log_weight, upper, preferred_element_type=F32, precision=lax.Precision.HIGHEST
    )
    lc_ref[...] = log_cum
    reach_ref[...] = jnp.exp(log_cum)
    lc_t[...] = jnp.concatenate([log_cum] * 8, axis=0).T
    om_t[...] = jnp.concatenate([1.0 / (1.0 + courant)] * 8, axis=0).T

    def build_transfer(radial, scale):
        row = lc_ref[pl.ds(radial, 1), :]
        lanes = lax.broadcasted_iota(jnp.int32, (SLOTS, LANES), 1)

        def body(block, carry):
            rows = pl.ds(pl.multiple_of(block * SLOTS, SLOTS), SLOTS)
            pick = lanes == radial
            lc_col = jnp.sum(jnp.where(pick, lc_t[rows, :], 0.0), axis=1, keepdims=True)
            om_col = jnp.sum(jnp.where(pick, om_t[rows, :], 0.0), axis=1, keepdims=True)
            source = block * SLOTS + lax.broadcasted_iota(jnp.int32, (SLOTS, CELLS), 0)
            cell = lax.broadcasted_iota(jnp.int32, (SLOTS, CELLS), 1)
            value = jnp.where(
                source <= cell, (om_col * scale) * jnp.exp(jnp.minimum(row - lc_col, 0.0)), 0.0
            )
            high, low = split(value)
            tcat[rows, :] = high
            tcat[pl.ds(pl.multiple_of(CELLS + block * SLOTS, SLOTS), SLOTS), :] = low
            tcat[pl.ds(pl.multiple_of(2 * CELLS + block * SLOTS, SLOTS), SLOTS), :] = high
            return carry

        lax.fori_loop(0, CELLS // SLOTS, body, 0)

    build_transfer(az, section_factor)

    pltpu.make_async_copy(mode_buf.at[pl.ds(0, NAZ - 1)], mode_buf.at[pl.ds(0, NAZ - 1)], m_recv).wait()
    first_lanes = lax.broadcasted_iota(jnp.int32, (8, LANES), 1) < SLOTS
    mode_lane = [
        jnp.where(first_lanes, mode_buf[2 * q], mode_buf[2 * q + 1]) for q in range(4)
    ]
    for q in range(4):
        wide = jnp.concatenate([mode_lane[q].astype(F32)] * 16, axis=0)
        mode_sub[pl.ds(q * LANES, LANES), :] = wide.T
    own_sub[...] = jnp.concatenate([mode_buf[az].astype(F32)] * 16, axis=0).T[:SLOTS, :]
    mode_row = jnp.concatenate(mode_lane, axis=1)[0:1, :]

    def tables(block, carry):
        rows = pl.ds(pl.multiple_of(block * 16, 16), 16)
        point = block * 16 + lax.broadcasted_iota(jnp.int32, (16, HALF), 0)
        cos_value, sin_value = cos_sin((mode_row * point) & (M - 1))
        for table, value in ((cos_f, cos_value), (sin_f, sin_value)):
            high, low = split(value)
            table[rows, 0:HALF] = high
            table[rows, HALF : 2 * HALF] = high
            table[rows, 2 * HALF : 3 * HALF] = low
        mode_col = mode_sub[rows, :].astype(jnp.int32)
        for q in range(4):
            lane_point = q * LANES + lax.broadcasted_iota(jnp.int32, (16, LANES), 1)
            cos_value, sin_value = cos_sin((mode_col * lane_point) & (M - 1))
            cos_value = jnp.where(lane_point == 0, 0.5 * cos_value, cos_value)
            for table, value in ((cos_r, cos_value), (sin_r, sin_value)):
                high, low = split(value)
                table[rows, q * LANES : (q + 1) * LANES] = high
                table[rows, HALF + q * LANES : HALF + (q + 1) * LANES] = high
                table[rows, 2 * HALF + q * LANES : 2 * HALF + (q + 1) * LANES] = low
        return carry

    lax.fori_loop(0, HALF // 16, tables, 0)

    def self_mode(block, carry):
        modes = mode_sub[pl.ds(pl.multiple_of(block * 8, 8), 8), :]
        return carry + modes * is_self(modes)

    first_self = jnp.sum(
        lax.fori_loop(0, HALF // 8, self_mode, jnp.zeros((8, LANES), F32)), axis=0, keepdims=True
    )
    second_is_half = first_self == 0.0
    norm = 1.0 / math.sqrt(M)

    def second_cos(rows, start):
        point = start + lax.broadcasted_iota(jnp.int32, (rows, LANES), 0)
        return jnp.where(second_is_half & ((point & 1) == 1), -norm, norm)

    def put_rhs(buf, block, lanes, value):
        high, low = split(value)
        start = block * SLOTS
        buf[pl.ds(pl.multiple_of(start, SLOTS), SLOTS), lanes] = high
        buf[pl.ds(pl.multiple_of(HALF + start, SLOTS), SLOTS), lanes] = low
        buf[pl.ds(pl.multiple_of(2 * HALF + start, SLOTS), SLOTS), lanes] = high

    def forward(chunk, carry):
        own_copy(chunk).wait()
        arrived = x_buf.at[chunk, :, pl.ds(0, (NAZ - 1) * SLOTS), :]
        pltpu.make_async_copy(arrived, arrived, f_recv.at[chunk]).wait()

        def fold(block, sums):
            modes = mode_sub[pl.ds(pl.multiple_of(block * SLOTS, SLOTS), SLOTS), :]
            alone = is_self(modes)
            parity = jnp.where((modes.astype(jnp.int32) & 1) == 1, -norm, norm)
            out = []
            for comp in range(4):
                one = x_buf[chunk, comp, pl.ds(pl.multiple_of(block * SLOTS, SLOTS), SLOTS), :]
                two = x_buf[chunk, comp, pl.ds(pl.multiple_of(HALF + block * SLOTS, SLOTS), SLOTS), :]
                even = one + (1.0 - alone) * two
                odd = (one - two) if comp % 2 == 1 else (two - one)
                put_rhs(rhs_a, block, pl.ds(comp * LANES, LANES), even)
                put_rhs(rhs_b, block, pl.ds((comp ^ 1) * LANES, LANES), odd)
                out.append(sums[comp] + fold_rows(alone * two))
                out.append(sums[4 + comp] + fold_rows(parity * even))
            return tuple(out[0::2] + out[1::2])

        zero = jnp.zeros((8, LANES), F32)
        sums = lax.fori_loop(0, HALF // SLOTS, fold, (zero,) * 8)
        alone_rows = [jnp.sum(sums[c], axis=0, keepdims=True) for c in range(4)]
        for c in range(4):
            middle = jnp.sum(sums[4 + c], axis=0, keepdims=True) + alone_rows[c] * norm
            fmid[chunk, c] = jnp.broadcast_to(middle, (8, LANES))
        for pair in range(2):
            lanes = slice(pair * 2 * LANES, (pair + 1) * 2 * LANES)
            fp[chunk, 2 * pair : 2 * pair + 2] = jnp.stack(
                jnp.split(
                    jnp.dot(cos_f[...], rhs_a[:, lanes], preferred_element_type=F32), 2, axis=1
                )
            )
            fm[chunk, 2 * pair : 2 * pair + 2] = jnp.stack(
                jnp.split(
                    jnp.dot(sin_f[...], rhs_b[:, lanes], preferred_element_type=F32), 2, axis=1
                )
            )

        def combine(block, carry):
            rows = pl.ds(pl.multiple_of(block * SLOTS, SLOTS), SLOTS)
            second = second_cos(SLOTS, block * SLOTS)
            for c in range(4):
                even = fp[chunk, c, rows, :] + second * alone_rows[c]
                odd = fm[chunk, c, rows, :]
                fp[chunk, c, rows, :] = even - odd
                fm[chunk, c, rows, :] = even + odd
            return carry

        lax.fori_loop(0, HALF // SLOTS, combine, 0)
        return carry

    lax.fori_loop(0, 2, forward, 0)

    lane64 = lax.broadcasted_iota(jnp.int32, (SLOTS, LANES), 1)
    lane8 = lax.broadcasted_iota(jnp.int32, (8, LANES), 1)

    def edges(block, carry):
        rows = pl.ds(pl.multiple_of(block * SLOTS, SLOTS), SLOTS)
        for side, chunk, lane in ((0, 1, LANES - 1), (1, 0, 0)):
            tile = jnp.zeros((SLOTS, LANES), F32)
            for c in range(4):
                tile = jnp.where(lane64 == c, fp[chunk, c, rows, lane : lane + 1], tile)
                tile = jnp.where(lane64 == 4 + c, fm[chunk, c, rows, lane : lane + 1], tile)
            halo_send[side, rows, :] = tile
        return carry

    lax.fori_loop(0, HALF // SLOTS, edges, 0)
    for side, chunk, lane in ((0, 1, LANES - 1), (1, 0, 0)):
        tile = jnp.zeros((8, LANES), F32)
        for c in range(4):
            tile = jnp.where(lane8 == c, fmid[chunk, c, :, lane : lane + 1], tile)
        halo_send[side, pl.ds(HALF, 8), :] = tile

    def halo_copy(side):
        return pltpu.make_async_remote_copy(
            src_ref=halo_send.at[side], dst_ref=halo_recv.at[side],
            send_sem=h_send.at[side], recv_sem=h_recv.at[side],
            device_id=(ax_target(1 if side == 0 else NAX - 1), az), device_id_type=MESH,
        )

    halo_copy(0).start()
    halo_copy(1).start()
    halo_copy(0).wait()
    halo_copy(1).wait()
    left_on = jnp.where(ax > 0, 1.0, 0.0)
    right_on = jnp.where(ax < NAX - 1, 1.0, 0.0)
    here = inverse_radius(az)
    here_square = here * here

    def flux_pair(get, rows, c, left_lane0, left_lanec, cell):
        first = jnp.concatenate([get(0, 0), get(1, 0)], axis=1)
        this = jnp.concatenate([get(0, c), get(1, c)], axis=1)
        third = jnp.concatenate([get(0, 2), get(1, 2)], axis=1)
        axial = first * this
        after = pltpu.roll(axial, CELLS - 1, axis=1)
        before = pltpu.roll(axial, 1, axis=1)
        left, right = left_lane0, left_lanec
        before = jnp.where(cell == 0, left, before)
        after = jnp.where(cell == CELLS - 1, right, after)
        return (before - after) * 0.5, third * this

    def pick_lane(tile, lanes, index):
        return jnp.sum(jnp.where(lanes == index, tile, 0.0), axis=1, keepdims=True)

    def explicit(c, carry):
        def fluxes(block, sums):
            rows = pl.ds(pl.multiple_of(block * SLOTS, SLOTS), SLOTS)
            cell = lax.broadcasted_iota(jnp.int32, (SLOTS, CELLS), 1)
            tile_l = halo_recv[0, rows, :]
            tile_r = halo_recv[1, rows, :]
            both = []
            for shift, source in ((0, fp), (4, fm)):
                left = tile_l[:, shift : shift + 1] * pick_lane(tile_l, lane64, c + shift) * left_on
                right = tile_r[:, shift : shift + 1] * pick_lane(tile_r, lane64, c + shift) * right_on
                both.append(
                    flux_pair(
                        lambda chunk, field, source=source: source[chunk, field, rows, :],
                        rows, c, left, right, cell,
                    )
                )
            (div_p, azi_p), (div_m, azi_m) = both
            div_even = div_p + div_m
            put_rhs(rhs_a, block, pl.ds(0, CELLS), div_even)
            put_rhs(rhs_a, block, pl.ds(CELLS, CELLS), azi_p + azi_m)
            put_rhs(rhs_b, block, pl.ds(0, CELLS), div_p - div_m)
            put_rhs(rhs_b, block, pl.ds(CELLS, CELLS), azi_p - azi_m)
            second = second_cos(SLOTS, block * SLOTS)
            point = block * SLOTS + lax.broadcasted_iota(jnp.int32, (SLOTS, LANES), 0)
            second = jnp.where(point == 0, 0.5 * second, second)
            second = jnp.concatenate([second, second], axis=1)
            return sums + fold_rows(second * div_even)

        second_sum = lax.fori_loop(0, HALF // SLOTS, fluxes, jnp.zeros((8, CELLS), F32))
        tile_l = halo_recv[0, pl.ds(HALF, 8), :]
        tile_r = halo_recv[1, pl.ds(HALF, 8), :]
        cell = lax.broadcasted_iota(jnp.int32, (8, CELLS), 1)
        div_mid, azi_mid = flux_pair(
            lambda chunk, field: fmid[chunk, field], None, c,
            tile_l[:, 0:1] * pick_lane(tile_l, lane8, c) * left_on,
            tile_r[:, 0:1] * pick_lane(tile_r, lane8, c) * right_on,
            cell,
        )
        div_mid = div_mid[0:1, :]
        azi_mid = azi_mid[0:1, :]
        second_row = jnp.sum(second_sum, axis=0, keepdims=True) + div_mid * norm

        for half in range(2):
            lanes = slice(half * CELLS, (half + 1) * CELLS)
            e_raw[half] = jnp.dot(cos_r[...], rhs_a[:, lanes], preferred_element_type=F32)
            e_raw[2 + half] = jnp.dot(sin_r[...], rhs_b[:, lanes], preferred_element_type=F32)

        def finish(block, carry):
            rows = pl.ds(pl.multiple_of(block * SLOTS, SLOTS), SLOTS)
            modes = mode_sub[rows, :]
            parity = jnp.where((modes.astype(jnp.int32) & 1) == 1, -norm, norm)
            wave = signed(modes) * here_square
            alone = is_self(modes)
            parity, wave, alone = (jnp.concatenate([v, v], axis=1) for v in (parity, wave, alone))
            cos_div = e_raw[0, rows, :] + parity * div_mid
            cos_azi = e_raw[1, rows, :] + parity * azi_mid
            real = cos_div - wave * e_raw[3, rows, :]
            imag = alone * second_row - e_raw[2, rows, :] - wave * cos_azi
            for part, value in ((0, real), (1, imag)):
                high, low = split(value)
                where = pl.ds(pl.multiple_of(part * HALF + block * SLOTS, SLOTS), SLOTS)
                lhs_cat[where, 0:CELLS] = high
                lhs_cat[where, CELLS : 2 * CELLS] = high
                lhs_cat[where, 2 * CELLS : 3 * CELLS] = low
            return carry

        lax.fori_loop(0, HALF // SLOTS, finish, 0)
        for part in range(2):
            e_send[c, part] = jnp.dot(
                lhs_cat[part * HALF : (part + 1) * HALF, :], tcat[...], preferred_element_type=F32
            )
        pltpu.make_async_copy(
            e_send.at[c, :, pl.ds(lax.rem(az, 8) * SLOTS, SLOTS), :], e_recv.at[c, az], own_e.at[c]
        ).start()

        for part in range(2):

            def send_back(offset, carry, part=part):
                target = az_target(offset)
                pltpu.make_async_remote_copy(
                    src_ref=e_send.at[c, part, pl.ds(lax.rem(target, 8) * SLOTS, SLOTS), :],
                    dst_ref=e_recv.at[c, az, part],
                    send_sem=e_send_sem, recv_sem=e_recv_sem.at[c],
                    device_id=(ax, target), device_id_type=MESH,
                ).start()
                return carry

            lax.fori_loop(1, NAZ, send_back, 0)
        return carry

    lax.fori_loop(0, FIELDS, explicit, 0)

    def state_sweep(radial, carry):
        build_transfer(radial, 1.0)
        there = inverse_radius(radial)
        ratio = signed(own_sub[...]) * there
        keep = 1.0 - (section_factor * viscosity) * ratio * ratio
        keep = jnp.concatenate([keep, keep], axis=1)
        for c in range(FIELDS):
            for part in range(2):
                high, low = split(st[radial, c, part] * keep)
                rows = pl.ds((2 * c + part) * SLOTS, SLOTS)
                lhs_cat[rows, 0:CELLS] = high
                lhs_cat[rows, CELLS : 2 * CELLS] = high
                lhs_cat[rows, 2 * CELLS : 3 * CELLS] = low
        swept = jnp.dot(lhs_cat[0:HALF, :], tcat[...], preferred_element_type=F32)
        st[radial] = swept.reshape(FIELDS, 2, SLOTS, CELLS)
        return carry

    lax.fori_loop(0, NR, state_sweep, 0)

    low_half = jnp.where(z < 2, 1.0, 0.0)
    own_alone = is_self(own_sub[...])
    swap = own_alone * (1.0 - low_half)
    flip = (1.0 - own_alone) * (2.0 * low_half - 1.0)
    swap = jnp.concatenate([swap, swap], axis=1)
    flip = jnp.concatenate([flip, flip], axis=1)

    def arrive(c, last):
        pltpu.make_async_copy(
            e_send.at[c, :, pl.ds(lax.rem(az, 8) * SLOTS, SLOTS), :], e_recv.at[c, az], own_e.at[c]
        ).wait()
        arrived = e_recv.at[c, pl.ds(0, NAZ - 1)]
        pltpu.make_async_copy(arrived, arrived, e_recv_sem.at[c]).wait()

        def add(radial, last):
            real = e_recv[c, radial, 0]
            imag = e_recv[c, radial, 1]
            new_real = st[radial, c, 0] + real + swap * (imag - real)
            new_imag = st[radial, c, 1] + flip * imag
            st[radial, c, 0] = new_real
            st[radial, c, 1] = new_imag
            where = c * 2 * NR + radial
            last = jnp.where(lane64 == where, new_real[:, CELLS - 1 : CELLS], last)
            last = jnp.where(lane64 == where + NR, new_imag[:, CELLS - 1 : CELLS], last)
            pltpu.make_async_copy(st.at[radial, c], acc_ref.at[c, :, radial], out_sem.at[c]).start()
            return last

        return lax.fori_loop(0, NR, add, last)

    last = lax.fori_loop(0, FIELDS, arrive, jnp.zeros((SLOTS, LANES), F32))

    rel_buf[ax, pl.ds(0, SLOTS), :] = last
    decay_row = jnp.exp(lc_t[pl.ds(CELLS - 8, 8), :])[7:8, :]
    rel_buf[ax, pl.ds(SLOTS, 8), :] = jnp.broadcast_to(decay_row, (8, LANES))

    def send_last(offset, carry):
        pltpu.make_async_remote_copy(
            src_ref=rel_buf.at[ax], dst_ref=rel_buf.at[ax], send_sem=rel_send, recv_sem=rel_recv,
            device_id=(ax_target(offset), az), device_id_type=MESH,
        ).start()
        return carry

    lax.fori_loop(1, NAX, send_last, 0)
    others = rel_buf.at[pl.ds(0, NAX - 1)]
    pltpu.make_async_copy(others, others, rel_recv).wait()

    def relay(block, incoming):
        upstream = rel_buf[block, pl.ds(0, SLOTS), :]
        decay = rel_buf[block, pl.ds(SLOTS, 8), :][0:1, :]
        return jnp.where(block < ax, decay * incoming + upstream, incoming)

    incoming_ref[...] = lax.fori_loop(0, NAX - 1, relay, inflow_ref[...])

    pltpu.make_async_copy(others, others, rel_send).wait()
    pltpu.make_async_copy(
        mode_buf.at[pl.ds(0, NAZ - 1)], mode_buf.at[pl.ds(0, NAZ - 1)], m_send
    ).wait()
    sent = send_buf.at[pl.ds(0, NAZ - 1)]
    pltpu.make_async_copy(sent, sent, f_send).wait()
    sent_back = e_recv.at[:, pl.ds(0, NAZ - 1)]
    pltpu.make_async_copy(sent_back, sent_back, e_send_sem).wait()

    def written(c, carry):
        pltpu.make_async_copy(acc_ref.at[c], acc_ref.at[c], out_sem.at[c]).wait()
        return carry

    lax.fori_loop(0, FIELDS, written, 0)


def shards(state, inflow, courant, mode_number, partner_table):
    modes = jnp.broadcast_to(jnp.concatenate([mode_number, mode_number])[None, :], (8, LANES))
    inflow_tile = inflow.reshape(FIELDS * 2 * NR, SLOTS).T
    dma = pltpu.SemaphoreType.DMA
    vmem = pltpu.VMEM
    acc, incoming, reach = pl.pallas_call(
        kernel,
        out_shape=(
            jax.ShapeDtypeStruct((FIELDS, 2, NR, SLOTS, CELLS), F32),
            jax.ShapeDtypeStruct((SLOTS, LANES), F32),
            jax.ShapeDtypeStruct((NR, CELLS), F32),
        ),
        in_specs=[
            pl.BlockSpec(memory_space=pl.ANY),
            pl.BlockSpec(memory_space=pltpu.VMEM),
            pl.BlockSpec(memory_space=pltpu.VMEM),
            pl.BlockSpec(memory_space=pltpu.VMEM),
        ],
        out_specs=(
            pl.BlockSpec(memory_space=pl.ANY),
            pl.BlockSpec(memory_space=pltpu.VMEM),
            pl.BlockSpec(memory_space=pltpu.VMEM),
        ),
        scratch_shapes=[
            vmem((NR, FIELDS, 2, SLOTS, CELLS), F32),
            vmem((NAZ, 2, 4, SLOTS, LANES), F32),
            vmem((2, 4, M, LANES), F32),
            vmem((NAZ, 8, LANES), jnp.int32),
            vmem((HALF, LANES), F32),
            vmem((SLOTS, LANES), F32),
            vmem((HALF, 3 * HALF), BF16),
            vmem((HALF, 3 * HALF), BF16),
            vmem((HALF, 3 * HALF), BF16),
            vmem((HALF, 3 * HALF), BF16),
            vmem((3 * HALF, 4 * LANES), BF16),
            vmem((3 * HALF, 4 * LANES), BF16),
            vmem((3 * CELLS, CELLS), BF16),
            vmem((2, FIELDS, HALF, LANES), F32),
            vmem((2, FIELDS, HALF, LANES), F32),
            vmem((2, FIELDS, 8, LANES), F32),
            vmem((8, LANES), F32),
            vmem((2, HALF + 8, LANES), F32),
            vmem((2, HALF + 8, LANES), F32),
            vmem((NR, CELLS), F32),
            vmem((CELLS, LANES), F32),
            vmem((CELLS, LANES), F32),
            vmem((4, HALF, CELLS), F32),
            vmem((FIELDS, 2, HALF, CELLS), F32),
            vmem((FIELDS, NAZ, 2, SLOTS, CELLS), F32),
            vmem((M, 3 * CELLS), BF16),
            vmem((NAX, SLOTS + 8, LANES), F32),
            dma((NAZ,)),
            dma,
            dma((2,)),
            dma,
            dma,
            dma((2,)),
            dma((2,)),
            dma((2,)),
            dma,
            dma((FIELDS,)),
            dma((FIELDS,)),
            dma((FIELDS,)),
            dma,
            dma,
        ],
        compiler_params=pltpu.CompilerParams(
            collective_id=0, has_side_effects=True, vmem_limit_bytes=58 * 2**20
        ),
    )(state, courant, modes, inflow_tile)
    incoming_full = incoming.T.reshape(FIELDS, 2, NR, SLOTS)
    return acc + reach[None, None, :, None, :] * incoming_full[..., None]


def solution(mesh):
    in_specs = (
        P(None, None, None, "az", "ax"),
        P(None, None, None, "az"),
        P(None, "ax"),
        P("az"),
        P("az"),
    )
    out_specs = P(None, None, None, "az", "ax")
    return jax.shard_map(shards, mesh=mesh, in_specs=in_specs, out_specs=out_specs, check_vma=False)
```

```python
import functools
import math

import jax
import jax.numpy as jnp
from jax import lax
from jax.experimental import pallas as pl
from jax.experimental.pallas import tpu as pltpu
from jax.sharding import PartitionSpec as P

section_factor = 0.5
viscosity = 0.02
M = 1024
HALF = M // 2
FIELDS = 4
NR = 16
SLOTS = 64
CELLS = 256
NAZ = 16
NAX = 8
LANES = 128
MESH = pl.DeviceIdType.MESH
F32 = jnp.float32
BF16 = jnp.bfloat16


def split(value):
    high = value.astype(BF16)
    low = (value - high.astype(F32)).astype(BF16)
    return high, low


def inverse_radius(radial_id):
    ratio = (0.6 + 0.4 * (radial_id.astype(F32) + 0.5) / NR) * (M / (2.0 * math.pi))
    return 1.0 / ratio


def cos_sin(phase):
    quadrant = lax.shift_right_logical(phase + 128, 8)
    angle = (phase - quadrant * 256).astype(F32) * (2.0 * math.pi / M)
    square = angle * angle
    sine = angle * (
        1.0
        + square
        * (-1.0 / 6 + square * (1.0 / 120 + square * (-1.0 / 5040 + square * (1.0 / 362880))))
    )
    cosine = 1.0 + square * (
        -0.5 + square * (1.0 / 24 + square * (-1.0 / 720 + square * (1.0 / 40320)))
    )
    odd = (quadrant & 1) == 1
    norm = 1.0 / math.sqrt(M)
    cos_value = jnp.where(odd, sine, cosine)
    sin_value = jnp.where(odd, cosine, sine)
    cos_sign = jnp.where(((quadrant + 1) & 2) == 2, -norm, norm)
    sin_sign = jnp.where((quadrant & 2) == 2, -norm, norm)
    return cos_value * cos_sign, sin_value * sin_sign


def signed(modes):
    return jnp.where(modes < HALF, modes, jnp.where(modes == HALF, 0.0, modes - M))


def is_self(modes):
    return jnp.where((modes == 0.0) | (modes == float(HALF)), 1.0, 0.0)


def fold_rows(value):
    rows, lanes = value.shape
    return jnp.sum(value.reshape(rows // 8, 8, lanes), axis=0)


def kernel(
    state_ref, courant_ref, mode_ref, inflow_ref,
    acc_ref, incoming_ref, reach_ref,
    st, send_buf, x_buf, mode_buf, mode_sub, own_sub,
    cos_f, sin_f, cos_r, sin_r, rhs_a, rhs_b, tcat,
    fp, fm, fmid, halo_send, halo_recv,
    lc_ref, lc_t, om_t, e_raw, e_send, e_recv, lhs_cat, rel_buf,
    st_sem, f_send, f_recv, m_send, m_recv, own_x, h_send, h_recv,
    e_send_sem, e_recv_sem, own_e, out_sem, rel_send, rel_recv,
):
    ax = lax.axis_index("ax")
    az = lax.axis_index("az")
    z = lax.div(az, 4)
    y = lax.rem(az, 4)

    def az_target(offset):
        step = lax.rem(offset * 7, NAZ)
        return lax.rem(z + lax.div(step, 4), 4) * 4 + lax.rem(y + lax.rem(step, 4), 4)

    def ax_target(offset):
        return lax.rem(ax + offset, NAX)

    def start_state(offset, carry):
        target = az_target(offset)
        pltpu.make_async_copy(
            state_ref.at[:, :, target], st.at[target], st_sem.at[target]
        ).start()
        return carry

    lax.fori_loop(0, NAZ, start_state, 0)

    barrier = pltpu.get_barrier_semaphore()

    def greet_az(offset, carry):
        pl.semaphore_signal(barrier, inc=1, device_id=(ax, az_target(offset)), device_id_type=MESH)
        return carry

    def greet_ax(offset, carry):
        pl.semaphore_signal(barrier, inc=1, device_id=(ax_target(offset), az), device_id_type=MESH)
        return carry

    lax.fori_loop(1, NAZ, greet_az, 0)
    lax.fori_loop(1, NAX, greet_ax, 0)

    modes_here = mode_ref[...]
    mode_buf[az] = jnp.broadcast_to(jnp.concatenate([modes_here, modes_here], axis=1), (8, LANES))

    def pack(offset, carry):
        target = az_target(offset)
        pltpu.make_async_copy(
            state_ref.at[:, :, target], st.at[target], st_sem.at[target]
        ).wait()
        low_lanes = lax.broadcasted_iota(jnp.int32, (SLOTS, LANES), 1) < LANES // 2
        for pair in range(2):
            one, two = 2 * pair, 2 * pair + 1
            values = []
            for tile in range(2):
                cells = pl.ds(tile * LANES, LANES)
                values.append(
                    (
                        st[target, one, 0, :, cells] - st[target, two, 1, :, cells],
                        st[target, one, 1, :, cells] + st[target, two, 0, :, cells],
                    )
                )
            for comp in range(2):
                first, second = values[0][comp], values[1][comp]
                send_buf[target, 0, pair, comp] = jnp.where(low_lanes, first, second)
                send_buf[target, 1, pair, comp] = jnp.where(low_lanes, second, first)
        return carry

    early = 6
    lax.fori_loop(0, early, pack, 0)
    pl.semaphore_wait(barrier, NAZ - 1 + NAX - 1)

    def send_modes(offset, carry):
        pltpu.make_async_remote_copy(
            src_ref=mode_buf.at[az], dst_ref=mode_buf.at[az], send_sem=m_send, recv_sem=m_recv,
            device_id=(ax, az_target(offset)), device_id_type=MESH,
        ).start()
        return carry

    lax.fori_loop(1, NAZ, send_modes, 0)

    def send_piece(target, chunk, pair, comp):
        pltpu.make_async_remote_copy(
            src_ref=send_buf.at[target, chunk, pair, comp],
            dst_ref=x_buf.at[chunk, pair, comp, pl.ds(az * SLOTS, SLOTS), :],
            send_sem=f_send, recv_sem=f_recv.at[2 * chunk + pair],
            device_id=(ax, target), device_id_type=MESH,
        ).start()

    def send_first(offset, carry):
        send_piece(az_target(offset), 0, 0, 0)
        return carry

    lax.fori_loop(1, early, send_first, 0)

    def pack_send(offset, carry):
        pack(offset, carry)
        return send_first(offset, carry)

    lax.fori_loop(early, NAZ, pack_send, 0)

    def send_rest(piece, carry):
        def send_more(offset, carry):
            send_piece(az_target(offset), lax.div(piece, 4), lax.rem(lax.div(piece, 2), 2), lax.rem(piece, 2))
            return carry

        return lax.fori_loop(1, NAZ, send_more, carry)

    lax.fori_loop(1, 8, send_rest, 0)

    own_copy = pltpu.make_async_copy(
        send_buf.at[az], x_buf.at[:, :, :, pl.ds(az * SLOTS, SLOTS), :], own_x
    )
    own_copy.start()

    courant = courant_ref[...]
    weight = courant / (1.0 + courant)
    gap = 1.0 - weight
    series = gap * (
        1.0 + gap * (1.0 / 2 + gap * (1.0 / 3 + gap * (1.0 / 4 + gap * (1.0 / 5 + gap * (1.0 / 6)))))
    )
    log_weight = jnp.where(gap < 0.05, -series, jnp.log(weight))
    row_ids = lax.broadcasted_iota(jnp.int32, (CELLS, CELLS), 0)
    col_ids = lax.broadcasted_iota(jnp.int32, (CELLS, CELLS), 1)
    upper = jnp.where(row_ids <= col_ids, 1.0, 0.0)
    log_cum = jnp.dot(
        log_weight, upper, preferred_element_type=F32, precision=lax.Precision.HIGHEST
    )
    lc_ref[...] = log_cum
    reach_ref[...] = jnp.exp(log_cum)
    lc_t[...] = jnp.concatenate([log_cum] * 8, axis=0).T
    om_t[...] = jnp.concatenate([gap] * 8, axis=0).T

    def build_transfer(radial, scale):
        row = lc_ref[pl.ds(radial, 1), :]
        lanes = lax.broadcasted_iota(jnp.int32, (SLOTS, LANES), 1)

        def body(block, carry):
            rows = pl.ds(pl.multiple_of(block * SLOTS, SLOTS), SLOTS)
            pick = lanes == radial
            lc_col = jnp.sum(jnp.where(pick, lc_t[rows, :], 0.0), axis=1, keepdims=True)
            om_col = jnp.sum(jnp.where(pick, om_t[rows, :], 0.0), axis=1, keepdims=True)
            source = block * SLOTS + lax.broadcasted_iota(jnp.int32, (SLOTS, CELLS), 0)
            cell = lax.broadcasted_iota(jnp.int32, (SLOTS, CELLS), 1)
            value = jnp.where(
                source <= cell, (om_col * scale) * jnp.exp(jnp.minimum(row - lc_col, 0.0)), 0.0
            )
            high, low = split(value)
            tcat[rows, :] = high
            tcat[pl.ds(pl.multiple_of(CELLS + block * SLOTS, SLOTS), SLOTS), :] = low
            tcat[pl.ds(pl.multiple_of(2 * CELLS + block * SLOTS, SLOTS), SLOTS), :] = high
            return carry

        lax.fori_loop(0, CELLS // SLOTS, body, 0)

    build_transfer(az, section_factor)

    pltpu.make_async_copy(mode_buf.at[pl.ds(0, NAZ - 1)], mode_buf.at[pl.ds(0, NAZ - 1)], m_recv).wait()
    first_lanes = lax.broadcasted_iota(jnp.int32, (8, LANES), 1) < SLOTS
    mode_lane = [
        jnp.where(first_lanes, mode_buf[2 * q], mode_buf[2 * q + 1]) for q in range(4)
    ]
    for q in range(4):
        wide = jnp.concatenate([mode_lane[q].astype(F32)] * 16, axis=0)
        mode_sub[pl.ds(q * LANES, LANES), :] = wide.T
    own_sub[...] = jnp.concatenate([mode_buf[az].astype(F32)] * 16, axis=0).T[:SLOTS, :]
    mode_row = jnp.concatenate(mode_lane, axis=1)[0:1, :]

    def tables(block, carry):
        rows = pl.ds(pl.multiple_of(block * 16, 16), 16)
        point = block * 16 + lax.broadcasted_iota(jnp.int32, (16, HALF), 0)
        cos_value, sin_value = cos_sin((mode_row * point) & (M - 1))
        for table, value in ((cos_f, cos_value), (sin_f, sin_value)):
            high, low = split(value)
            table[rows, 0:HALF] = high
            table[rows, HALF : 2 * HALF] = high
            table[rows, 2 * HALF : 3 * HALF] = low
        mode_col = mode_sub[rows, :].astype(jnp.int32)
        for q in range(4):
            lane_point = q * LANES + lax.broadcasted_iota(jnp.int32, (16, LANES), 1)
            cos_value, sin_value = cos_sin((mode_col * lane_point) & (M - 1))
            cos_value = jnp.where(lane_point == 0, 0.5 * cos_value, cos_value)
            for table, value in ((cos_r, cos_value), (sin_r, sin_value)):
                high, low = split(value)
                table[rows, q * LANES : (q + 1) * LANES] = high
                table[rows, HALF + q * LANES : HALF + (q + 1) * LANES] = high
                table[rows, 2 * HALF + q * LANES : 2 * HALF + (q + 1) * LANES] = low
        return carry

    lax.fori_loop(0, HALF // 16, tables, 0)

    def self_mode(block, carry):
        modes = mode_sub[pl.ds(pl.multiple_of(block * 8, 8), 8), :]
        return carry + modes * is_self(modes)

    first_self = jnp.sum(
        lax.fori_loop(0, HALF // 8, self_mode, jnp.zeros((8, LANES), F32)), axis=0, keepdims=True
    )
    second_is_half = first_self == 0.0
    norm = 1.0 / math.sqrt(M)

    def second_cos(rows, start):
        point = start + lax.broadcasted_iota(jnp.int32, (rows, LANES), 0)
        return jnp.where(second_is_half & ((point & 1) == 1), -norm, norm)

    def put_rhs(buf, block, lanes, value):
        high, low = split(value)
        start = block * SLOTS
        buf[pl.ds(pl.multiple_of(start, SLOTS), SLOTS), lanes] = high
        buf[pl.ds(pl.multiple_of(HALF + start, SLOTS), SLOTS), lanes] = low
        buf[pl.ds(pl.multiple_of(2 * HALF + start, SLOTS), SLOTS), lanes] = high

    lane64 = lax.broadcasted_iota(jnp.int32, (SLOTS, LANES), 1)
    lane8 = lax.broadcasted_iota(jnp.int32, (8, LANES), 1)
    own_copy.wait()

    def halo_copy(side):
        return pltpu.make_async_remote_copy(
            src_ref=halo_send.at[side], dst_ref=halo_recv.at[side],
            send_sem=h_send.at[side], recv_sem=h_recv.at[side],
            device_id=(ax_target(1 if side == 0 else NAX - 1), az), device_id_type=MESH,
        )

    def send_edges():
        def edges(block, carry):
            rows = pl.ds(pl.multiple_of(block * SLOTS, SLOTS), SLOTS)
            for side, lane in ((0, LANES - 1), (1, 0)):
                tile = jnp.zeros((SLOTS, LANES), F32)
                for c in range(4):
                    tile = jnp.where(lane64 == c, fp[0, c, rows, lane : lane + 1], tile)
                    tile = jnp.where(lane64 == 4 + c, fm[0, c, rows, lane : lane + 1], tile)
                halo_send[side, rows, :] = tile
            return carry

        lax.fori_loop(0, HALF // SLOTS, edges, 0)
        for side, lane in ((0, LANES - 1), (1, 0)):
            tile = jnp.zeros((8, LANES), F32)
            for c in range(4):
                tile = jnp.where(lane8 == c, fmid[0, c, :, lane : lane + 1], tile)
            halo_send[side, pl.ds(HALF, 8), :] = tile
        halo_copy(0).start()
        halo_copy(1).start()

    def forward(unit, carry):
        chunk = lax.div(unit, 2)
        pair = lax.rem(unit, 2)
        arrived = x_buf.at[chunk, pair, :, pl.ds(0, (NAZ - 1) * SLOTS), :]
        pltpu.make_async_copy(arrived, arrived, f_recv.at[unit]).wait()

        def fold(block, sums):
            modes = mode_sub[pl.ds(pl.multiple_of(block * SLOTS, SLOTS), SLOTS), :]
            alone = is_self(modes)
            parity = jnp.where((modes.astype(jnp.int32) & 1) == 1, -norm, norm)
            out = []
            for comp in range(2):
                one = x_buf[chunk, pair, comp, pl.ds(pl.multiple_of(block * SLOTS, SLOTS), SLOTS), :]
                two = x_buf[
                    chunk, pair, comp, pl.ds(pl.multiple_of(HALF + block * SLOTS, SLOTS), SLOTS), :
                ]
                even = one + (1.0 - alone) * two
                odd = (one - two) if comp % 2 == 1 else (two - one)
                put_rhs(rhs_a, block, pl.ds(comp * LANES, LANES), even)
                put_rhs(rhs_b, block, pl.ds((comp ^ 1) * LANES, LANES), odd)
                out.append(sums[comp] + fold_rows(alone * two))
                out.append(sums[2 + comp] + fold_rows(parity * even))
            return tuple(out[0::2] + out[1::2])

        zero = jnp.zeros((8, LANES), F32)
        sums = lax.fori_loop(0, HALF // SLOTS, fold, (zero,) * 4)
        alone_rows = [jnp.sum(sums[c], axis=0, keepdims=True) for c in range(2)]
        for c in range(2):
            middle = jnp.sum(sums[2 + c], axis=0, keepdims=True) + alone_rows[c] * norm
            fmid[chunk, 2 * pair + c] = jnp.broadcast_to(middle, (8, LANES))
        cos_sum = jnp.dot(cos_f[...], rhs_a[:, 0:CELLS], preferred_element_type=F32)
        sin_sum = jnp.dot(sin_f[...], rhs_b[:, 0:CELLS], preferred_element_type=F32)
        for c in range(2):
            lanes = slice(c * LANES, (c + 1) * LANES)
            fp[chunk, 2 * pair + c] = cos_sum[:, lanes]
            fm[chunk, 2 * pair + c] = sin_sum[:, lanes]

        def combine(block, carry):
            rows = pl.ds(pl.multiple_of(block * SLOTS, SLOTS), SLOTS)
            second = second_cos(SLOTS, block * SLOTS)
            for c in range(2):
                even = fp[chunk, 2 * pair + c, rows, :] + second * alone_rows[c]
                odd = fm[chunk, 2 * pair + c, rows, :]
                fp[chunk, 2 * pair + c, rows, :] = even - odd
                fm[chunk, 2 * pair + c, rows, :] = even + odd
            return carry

        lax.fori_loop(0, HALF // SLOTS, combine, 0)

        @pl.when(unit == 1)
        def _():
            send_edges()

        return carry

    lax.fori_loop(0, 4, forward, 0)
    halo_copy(0).wait()
    halo_copy(1).wait()
    left_on = jnp.where(ax > 0, 1.0, 0.0)
    right_on = jnp.where(ax < NAX - 1, 1.0, 0.0)
    here = inverse_radius(az)
    here_square = here * here

    def flux_pair(get, rows, c, left_lane0, left_lanec, cell):
        def cells(field):
            outer, inner = get(0, field), get(1, field)
            low_lanes = (lane64 if rows is not None else lane8) < LANES // 2
            return jnp.concatenate(
                [jnp.where(low_lanes, outer, inner), jnp.where(low_lanes, inner, outer)], axis=1
            )

        first, this, third = cells(0), cells(c), cells(2)
        axial = first * this
        after = pltpu.roll(axial, CELLS - 1, axis=1)
        before = pltpu.roll(axial, 1, axis=1)
        left, right = left_lane0, left_lanec
        before = jnp.where(cell == 0, left, before)
        after = jnp.where(cell == CELLS - 1, right, after)
        return (before - after) * 0.5, third * this

    def pick_lane(tile, lanes, index):
        return jnp.sum(jnp.where(lanes == index, tile, 0.0), axis=1, keepdims=True)

    def own_back(c):
        return pltpu.make_async_copy(
            e_send.at[c, :, :, pl.ds(lax.rem(az, 8) * SLOTS, SLOTS), :],
            e_recv.at[c, :, az],
            own_e.at[c],
        )

    def explicit(c, carry):
        def fluxes(block, sums):
            rows = pl.ds(pl.multiple_of(block * SLOTS, SLOTS), SLOTS)
            cell = lax.broadcasted_iota(jnp.int32, (SLOTS, CELLS), 1)
            tile_l = halo_recv[0, rows, :]
            tile_r = halo_recv[1, rows, :]
            both = []
            for shift, source in ((0, fp), (4, fm)):
                left = tile_l[:, shift : shift + 1] * pick_lane(tile_l, lane64, c + shift) * left_on
                right = tile_r[:, shift : shift + 1] * pick_lane(tile_r, lane64, c + shift) * right_on
                both.append(
                    flux_pair(
                        lambda chunk, field, source=source: source[chunk, field, rows, :],
                        rows, c, left, right, cell,
                    )
                )
            (div_p, azi_p), (div_m, azi_m) = both
            div_even = div_p + div_m
            put_rhs(rhs_a, block, pl.ds(0, CELLS), div_even)
            put_rhs(rhs_a, block, pl.ds(CELLS, CELLS), azi_p + azi_m)
            put_rhs(rhs_b, block, pl.ds(0, CELLS), div_p - div_m)
            put_rhs(rhs_b, block, pl.ds(CELLS, CELLS), azi_p - azi_m)
            second = second_cos(SLOTS, block * SLOTS)
            point = block * SLOTS + lax.broadcasted_iota(jnp.int32, (SLOTS, LANES), 0)
            second = jnp.where(point == 0, 0.5 * second, second)
            second = jnp.concatenate([second, second], axis=1)
            return sums + fold_rows(second * div_even)

        second_sum = lax.fori_loop(0, HALF // SLOTS, fluxes, jnp.zeros((8, CELLS), F32))
        tile_l = halo_recv[0, pl.ds(HALF, 8), :]
        tile_r = halo_recv[1, pl.ds(HALF, 8), :]
        cell = lax.broadcasted_iota(jnp.int32, (8, CELLS), 1)
        div_mid, azi_mid = flux_pair(
            lambda chunk, field: fmid[chunk, field], None, c,
            tile_l[:, 0:1] * pick_lane(tile_l, lane8, c) * left_on,
            tile_r[:, 0:1] * pick_lane(tile_r, lane8, c) * right_on,
            cell,
        )
        div_mid = div_mid[0:1, :]
        azi_mid = azi_mid[0:1, :]
        second_row = jnp.sum(second_sum, axis=0, keepdims=True) + div_mid * norm

        for half in range(2):
            lanes = slice(half * CELLS, (half + 1) * CELLS)
            e_raw[half] = jnp.dot(cos_r[...], rhs_a[:, lanes], preferred_element_type=F32)
            e_raw[2 + half] = jnp.dot(sin_r[...], rhs_b[:, lanes], preferred_element_type=F32)

        def finish(block, carry):
            rows = pl.ds(pl.multiple_of(block * SLOTS, SLOTS), SLOTS)
            modes = mode_sub[rows, :]
            parity = jnp.where((modes.astype(jnp.int32) & 1) == 1, -norm, norm)
            wave = signed(modes) * here_square
            alone = is_self(modes)
            parity, wave, alone = (jnp.concatenate([v, v], axis=1) for v in (parity, wave, alone))
            cos_div = e_raw[0, rows, :] + parity * div_mid
            cos_azi = e_raw[1, rows, :] + parity * azi_mid
            real = cos_div - wave * e_raw[3, rows, :]
            imag = alone * second_row - e_raw[2, rows, :] - wave * cos_azi
            for part, value in ((0, real), (1, imag)):
                high, low = split(value)
                where = pl.ds(pl.multiple_of(part * HALF + block * SLOTS, SLOTS), SLOTS)
                lhs_cat[where, 0:CELLS] = high
                lhs_cat[where, CELLS : 2 * CELLS] = high
                lhs_cat[where, 2 * CELLS : 3 * CELLS] = low
            return carry

        lax.fori_loop(0, HALF // SLOTS, finish, 0)
        for part in range(2):
            swept = jnp.dot(
                lhs_cat[part * HALF : (part + 1) * HALF, :], tcat[...], preferred_element_type=F32
            )
            for tile in range(2):
                e_send[c, tile, part] = swept[:, tile * LANES : (tile + 1) * LANES]
        own_back(c).start()

        def send_piece_back(piece, carry):
            tile = 1 - lax.div(piece, 2)
            part = lax.rem(piece, 2)

            def send_back(offset, carry):
                target = az_target(offset)
                pltpu.make_async_remote_copy(
                    src_ref=e_send.at[c, tile, part, pl.ds(lax.rem(target, 8) * SLOTS, SLOTS), :],
                    dst_ref=e_recv.at[c, tile, az, part],
                    send_sem=e_send_sem, recv_sem=e_recv_sem.at[2 * c + tile],
                    device_id=(ax, target), device_id_type=MESH,
                ).start()
                return carry

            return lax.fori_loop(1, NAZ, send_back, carry)

        lax.fori_loop(0, 4, send_piece_back, 0)
        return carry

    lax.fori_loop(0, FIELDS, explicit, 0)

    def state_sweep(radial, carry):
        build_transfer(radial, 1.0)
        there = inverse_radius(radial)
        ratio = signed(own_sub[...]) * there
        keep = 1.0 - (section_factor * viscosity) * ratio * ratio
        keep = jnp.concatenate([keep, keep], axis=1)
        for c in range(FIELDS):
            for part in range(2):
                high, low = split(st[radial, c, part] * keep)
                rows = pl.ds((2 * c + part) * SLOTS, SLOTS)
                lhs_cat[rows, 0:CELLS] = high
                lhs_cat[rows, CELLS : 2 * CELLS] = high
                lhs_cat[rows, 2 * CELLS : 3 * CELLS] = low
        swept = jnp.dot(lhs_cat[0:HALF, :], tcat[...], preferred_element_type=F32)
        st[radial] = swept.reshape(FIELDS, 2, SLOTS, CELLS)
        return carry

    lax.fori_loop(0, NR, state_sweep, 0)

    low_half = jnp.where(z < 2, 1.0, 0.0)
    own_alone = is_self(own_sub[...])
    swap = own_alone * (1.0 - low_half)
    flip = (1.0 - own_alone) * (2.0 * low_half - 1.0)
    decay_row = jnp.exp(lc_t[pl.ds(CELLS - 8, 8), :])[7:8, :]
    rel_buf[ax, pl.ds(SLOTS, 8), :] = jnp.broadcast_to(decay_row, (8, LANES))

    def send_last(offset, carry):
        pltpu.make_async_remote_copy(
            src_ref=rel_buf.at[ax], dst_ref=rel_buf.at[ax], send_sem=rel_send, recv_sem=rel_recv,
            device_id=(ax_target(offset), az), device_id_type=MESH,
        ).start()
        return carry

    def arrive(c, last):
        own_back(c).wait()

        def add(tile, radial):
            lanes = pl.ds(tile * LANES, LANES)
            real = e_recv[c, tile, radial, 0]
            imag = e_recv[c, tile, radial, 1]
            new_real = st[radial, c, 0, :, lanes] + real + swap * (imag - real)
            new_imag = st[radial, c, 1, :, lanes] + flip * imag
            st[radial, c, 0, :, lanes] = new_real
            st[radial, c, 1, :, lanes] = new_imag
            return new_real, new_imag

        def landed(tile):
            ref = e_recv.at[c, tile, pl.ds(0, NAZ - 1)]
            pltpu.make_async_copy(ref, ref, e_recv_sem.at[2 * c + tile]).wait()

        def add_last(radial, last):
            new_real, new_imag = add(1, radial)
            where = c * 2 * NR + radial
            last = jnp.where(lane64 == where, new_real[:, LANES - 1 : LANES], last)
            return jnp.where(lane64 == where + NR, new_imag[:, LANES - 1 : LANES], last)

        def add_first(radial, carry):
            add(0, radial)
            pltpu.make_async_copy(st.at[radial, c], acc_ref.at[c, :, radial], out_sem.at[c]).start()
            return carry

        landed(1)
        last = lax.fori_loop(0, NR, add_last, last)

        @pl.when(c == FIELDS - 1)
        def _():
            rel_buf[ax, pl.ds(0, SLOTS), :] = last
            lax.fori_loop(1, NAX, send_last, 0)

        landed(0)
        lax.fori_loop(0, NR, add_first, 0)
        return last

    lax.fori_loop(0, FIELDS, arrive, jnp.zeros((SLOTS, LANES), F32))

    others = rel_buf.at[pl.ds(0, NAX - 1)]
    pltpu.make_async_copy(others, others, rel_recv).wait()

    def relay(block, incoming):
        upstream = rel_buf[block, pl.ds(0, SLOTS), :]
        decay = rel_buf[block, pl.ds(SLOTS, 8), :][0:1, :]
        return jnp.where(block < ax, decay * incoming + upstream, incoming)

    inflow = inflow_ref[...]
    inflow = jnp.concatenate([inflow, inflow], axis=1).T[:SLOTS, :]
    incoming = lax.fori_loop(0, NAX - 1, relay, inflow)
    incoming_ref[...] = jnp.concatenate([incoming, incoming], axis=0).T[:, :SLOTS]

    pltpu.make_async_copy(others, others, rel_send).wait()
    pltpu.make_async_copy(
        mode_buf.at[pl.ds(0, NAZ - 1)], mode_buf.at[pl.ds(0, NAZ - 1)], m_send
    ).wait()
    sent = send_buf.at[pl.ds(0, NAZ - 1)]
    pltpu.make_async_copy(sent, sent, f_send).wait()
    sent_back = e_recv.at[:, :, pl.ds(0, NAZ - 1)]
    pltpu.make_async_copy(sent_back, sent_back, e_send_sem).wait()

    def written(c, carry):
        pltpu.make_async_copy(acc_ref.at[c], acc_ref.at[c], out_sem.at[c]).wait()
        return carry

    lax.fori_loop(0, FIELDS, written, 0)


def shards(state, inflow, courant, mode_number, partner_table):
    modes = mode_number.reshape(1, SLOTS)
    inflow_rows = inflow.reshape(FIELDS * 2 * NR, SLOTS)
    dma = pltpu.SemaphoreType.DMA
    vmem = pltpu.VMEM
    acc, incoming, reach = pl.pallas_call(
        kernel,
        out_shape=(
            jax.ShapeDtypeStruct((FIELDS, 2, NR, SLOTS, CELLS), F32),
            jax.ShapeDtypeStruct((FIELDS * 2 * NR, SLOTS), F32),
            jax.ShapeDtypeStruct((NR, CELLS), F32),
        ),
        in_specs=[
            pl.BlockSpec(memory_space=pl.ANY),
            pl.BlockSpec(memory_space=pltpu.VMEM),
            pl.BlockSpec(memory_space=pltpu.VMEM),
            pl.BlockSpec(memory_space=pltpu.VMEM),
        ],
        out_specs=(
            pl.BlockSpec(memory_space=pl.ANY),
            pl.BlockSpec(memory_space=pltpu.VMEM),
            pl.BlockSpec(memory_space=pltpu.VMEM),
        ),
        scratch_shapes=[
            vmem((NR, FIELDS, 2, SLOTS, CELLS), F32),
            vmem((NAZ, 2, 2, 2, SLOTS, LANES), F32),
            vmem((2, 2, 2, M, LANES), F32),
            vmem((NAZ, 8, LANES), jnp.int32),
            vmem((HALF, LANES), F32),
            vmem((SLOTS, LANES), F32),
            vmem((HALF, 3 * HALF), BF16),
            vmem((HALF, 3 * HALF), BF16),
            vmem((HALF, 3 * HALF), BF16),
            vmem((HALF, 3 * HALF), BF16),
            vmem((3 * HALF, 4 * LANES), BF16),
            vmem((3 * HALF, 4 * LANES), BF16),
            vmem((3 * CELLS, CELLS), BF16),
            vmem((2, FIELDS, HALF, LANES), F32),
            vmem((2, FIELDS, HALF, LANES), F32),
            vmem((2, FIELDS, 8, LANES), F32),
            vmem((2, HALF + 8, LANES), F32),
            vmem((2, HALF + 8, LANES), F32),
            vmem((NR, CELLS), F32),
            vmem((CELLS, LANES), F32),
            vmem((CELLS, LANES), F32),
            vmem((4, HALF, CELLS), F32),
            vmem((FIELDS, 2, 2, HALF, LANES), F32),
            vmem((FIELDS, 2, NAZ, 2, SLOTS, LANES), F32),
            vmem((M, 3 * CELLS), BF16),
            vmem((NAX, SLOTS + 8, LANES), F32),
            dma((NAZ,)),
            dma,
            dma((4,)),
            dma,
            dma,
            dma,
            dma((2,)),
            dma((2,)),
            dma,
            dma((2 * FIELDS,)),
            dma((FIELDS,)),
            dma((FIELDS,)),
            dma,
            dma,
        ],
        compiler_params=pltpu.CompilerParams(
            collective_id=0, has_side_effects=True, vmem_limit_bytes=58 * 2**20
        ),
    )(state, courant, modes, inflow_rows)
    incoming_full = incoming.reshape(FIELDS, 2, NR, SLOTS)
    return acc + reach[None, None, :, None, :] * incoming_full[..., None]


def solution(mesh):
    in_specs = (
        P(None, None, None, "az", "ax"),
        P(None, None, None, "az"),
        P(None, "ax"),
        P("az"),
        P("az"),
    )
    out_specs = P(None, None, None, "az", "ax")
    return jax.shard_map(shards, mesh=mesh, in_specs=in_specs, out_specs=out_specs, check_vma=False)
```

```python
import functools
import math

import jax
import jax.numpy as jnp
from jax import lax
from jax.experimental import pallas as pl
from jax.experimental.pallas import tpu as pltpu
from jax.sharding import PartitionSpec as P

section_factor = 0.5
viscosity = 0.02
M = 1024
HALF = M // 2
FIELDS = 4
NR = 16
SLOTS = 64
CELLS = 256
NAZ = 16
NAX = 8
LANES = 128
MESH = pl.DeviceIdType.MESH
F32 = jnp.float32
BF16 = jnp.bfloat16


def split(value):
    high = value.astype(BF16)
    low = (value - high.astype(F32)).astype(BF16)
    return high, low


def inverse_radius(radial_id):
    ratio = (0.6 + 0.4 * (radial_id.astype(F32) + 0.5) / NR) * (M / (2.0 * math.pi))
    return 1.0 / ratio


def cos_sin(phase):
    quadrant = lax.shift_right_logical(phase + 128, 8)
    angle = (phase - quadrant * 256).astype(F32) * (2.0 * math.pi / M)
    square = angle * angle
    sine = angle * (
        1.0
        + square
        * (-1.0 / 6 + square * (1.0 / 120 + square * (-1.0 / 5040 + square * (1.0 / 362880))))
    )
    cosine = 1.0 + square * (
        -0.5 + square * (1.0 / 24 + square * (-1.0 / 720 + square * (1.0 / 40320)))
    )
    odd = (quadrant & 1) == 1
    norm = 1.0 / math.sqrt(M)
    cos_value = jnp.where(odd, sine, cosine)
    sin_value = jnp.where(odd, cosine, sine)
    cos_sign = jnp.where(((quadrant + 1) & 2) == 2, -norm, norm)
    sin_sign = jnp.where((quadrant & 2) == 2, -norm, norm)
    return cos_value * cos_sign, sin_value * sin_sign


def signed(modes):
    return jnp.where(modes < HALF, modes, jnp.where(modes == HALF, 0.0, modes - M))


def is_self(modes):
    return jnp.where((modes == 0.0) | (modes == float(HALF)), 1.0, 0.0)


def fold_rows(value):
    rows, lanes = value.shape
    return jnp.sum(value.reshape(rows // 8, 8, lanes), axis=0)


def kernel(
    state_ref, courant_ref, mode_ref, inflow_ref,
    acc_ref, incoming_ref, reach_ref,
    st, send_buf, x_buf, alone_send, alone_recv, alone_sum, mode_buf, mode_sub, own_sub,
    cos_f, sin_f, cos_r, sin_r, rhs_a, rhs_b, tcat,
    fp, fm, fmid, halo_send, halo_recv,
    lc_ref, lc_t, om_t, e_raw, e_send, e_recv, lhs_cat, rel_buf,
    st_sem, f_send, f_recv, a_send, a_recv, m_send, m_recv, own_x, h_send, h_recv,
    e_send_sem, e_recv_sem, own_e, out_sem, rel_send, rel_recv,
):
    ax = lax.axis_index("ax")
    az = lax.axis_index("az")
    z = lax.div(az, 4)
    y = lax.rem(az, 4)

    def az_target(offset):
        step = lax.rem(offset * 7, NAZ)
        return lax.rem(z + lax.div(step, 4), 4) * 4 + lax.rem(y + lax.rem(step, 4), 4)

    def ax_target(offset):
        return lax.rem(ax + offset, NAX)

    def start_state(offset, carry):
        turn = lax.div(offset, 4)
        step = lax.rem(1 + 2 * turn + lax.div(turn, 2) * 3, 4)
        target = lax.rem(z + step, 4) * 4 + lax.rem(y + lax.rem(offset, 4), 4)
        pltpu.make_async_copy(
            state_ref.at[:, :, target], st.at[target], st_sem.at[target]
        ).start()
        return carry

    lax.fori_loop(0, NAZ, start_state, 0)

    barrier = pltpu.get_barrier_semaphore()

    def greet_az(offset, carry):
        pl.semaphore_signal(barrier, inc=1, device_id=(ax, az_target(offset)), device_id_type=MESH)
        return carry

    def greet_ax(offset, carry):
        pl.semaphore_signal(barrier, inc=1, device_id=(ax_target(offset), az), device_id_type=MESH)
        return carry

    lax.fori_loop(1, NAZ, greet_az, 0)
    lax.fori_loop(1, NAX, greet_ax, 0)

    modes_here = mode_ref[...]
    mode_buf[az] = jnp.broadcast_to(jnp.concatenate([modes_here, modes_here], axis=1), (8, LANES))

    own_sub[...] = jnp.concatenate([mode_buf[az].astype(F32)] * 16, axis=0).T[:SLOTS, :]

    group = lax.rem(z, 2) * 4 + y
    sign = jnp.where(z < 2, 1.0, -1.0)
    low_lanes = lax.broadcasted_iota(jnp.int32, (SLOTS, LANES), 1) < LANES // 2

    def column(step, dy):
        return lax.rem(z + step, 4) * 4 + lax.rem(y + dy, 4)

    def state_here(target):
        pltpu.make_async_copy(
            state_ref.at[:, :, target], st.at[target], st_sem.at[target]
        ).wait()

    def pack(step, parts):
        def body(dy, carry):
            target = column(step, dy)
            state_here(target)
            for field in range(FIELDS):
                for part in parts:
                    first = st[target, field, part, :, 0:LANES]
                    second = st[target, field, part, :, LANES:CELLS]
                    if part == 1:
                        first, second = first * sign, second * sign
                    pair, place = field % 2, field // 2
                    send_buf[target, 0, pair, place, part] = jnp.where(low_lanes, first, second)
                    send_buf[target, 1, pair, place, part] = jnp.where(low_lanes, second, first)
            return carry

        lax.fori_loop(0, 4, body, 0)

    pack(1, (0,))
    pack(3, (1,))
    pl.semaphore_wait(barrier, NAZ - 1 + NAX - 1)

    def send_modes(offset, carry):
        pltpu.make_async_remote_copy(
            src_ref=mode_buf.at[az], dst_ref=mode_buf.at[az], send_sem=m_send, recv_sem=m_recv,
            device_id=(ax, az_target(offset)), device_id_type=MESH,
        ).start()
        return carry

    lax.fori_loop(1, NAZ, send_modes, 0)

    def send_piece(chunk, pair, place, index):
        same = lax.div(index, 8)
        part = (1 - same) * lax.div(index, 4) + same * lax.rem(index, 2)
        step = (1 - same) * (1 + 2 * lax.div(index, 4))
        dy = (1 - same) * lax.rem(index, 4) + same * (lax.div(index, 2) - 3)
        target = column(step, dy)
        pltpu.make_async_remote_copy(
            src_ref=send_buf.at[target, chunk, pair, place, part],
            dst_ref=x_buf.at[chunk, pair, place, part, pl.ds(group * SLOTS, SLOTS), :],
            send_sem=f_send, recv_sem=f_recv.at[2 * chunk + pair],
            device_id=(ax, target), device_id_type=MESH,
        ).start()

    def send_first(index, carry):
        send_piece(0, 0, 0, index)
        return carry

    lax.fori_loop(0, 8, send_first, 0)
    pack(0, (0, 1))
    lax.fori_loop(8, 14, send_first, 0)

    def send_rest(piece, carry):
        def send_more(count, carry):
            send_piece(
                lax.div(piece, 4), lax.rem(lax.div(piece, 2), 2), lax.rem(piece, 2),
                lax.rem(count * 5, 14),
            )
            return carry

        return lax.fori_loop(0, 14, send_more, carry)

    lax.fori_loop(1, 2, send_rest, 0)

    own_alone = is_self(own_sub[...])

    def alone_there(dy, carry):
        state_here(column(2, dy))
        return carry

    lax.fori_loop(0, 4, alone_there, 0)

    def alone_row(radial, carry):
        rows = [[], []]
        for field in range(FIELDS):
            first = jnp.sum(own_alone * st[radial, field, 0, :, 0:LANES], axis=0, keepdims=True)
            second = jnp.sum(own_alone * st[radial, field, 0, :, LANES:CELLS], axis=0, keepdims=True)
            rows[0].append(jnp.where(low_lanes[0:1], first, second))
            rows[1].append(jnp.where(low_lanes[0:1], second, first))
        alone_send[radial] = jnp.concatenate(rows[0] + rows[1], axis=0)
        return carry

    lax.fori_loop(0, NR, alone_row, 0)
    alone_recv[az] = alone_send[az]

    def send_alone(offset, carry):
        target = az_target(offset)
        pltpu.make_async_remote_copy(
            src_ref=alone_send.at[target], dst_ref=alone_recv.at[az], send_sem=a_send,
            recv_sem=a_recv, device_id=(ax, target), device_id_type=MESH,
        ).start()
        return carry

    lax.fori_loop(1, NAZ, send_alone, 0)
    lax.fori_loop(2, 8, send_rest, 0)

    own_copy = pltpu.make_async_copy(
        send_buf.at[az], x_buf.at[:, :, :, :, pl.ds(group * SLOTS, SLOTS), :], own_x
    )
    own_copy.start()

    courant = courant_ref[...]
    weight = courant / (1.0 + courant)
    gap = 1.0 - weight
    series = gap * (
        1.0 + gap * (1.0 / 2 + gap * (1.0 / 3 + gap * (1.0 / 4 + gap * (1.0 / 5 + gap * (1.0 / 6)))))
    )
    log_weight = jnp.where(gap < 0.05, -series, jnp.log(weight))
    row_ids = lax.broadcasted_iota(jnp.int32, (CELLS, CELLS), 0)
    col_ids = lax.broadcasted_iota(jnp.int32, (CELLS, CELLS), 1)
    upper = jnp.where(row_ids <= col_ids, 1.0, 0.0)
    log_cum = jnp.dot(
        log_weight, upper, preferred_element_type=F32, precision=lax.Precision.HIGHEST
    )
    lc_ref[...] = log_cum
    reach_ref[...] = jnp.exp(log_cum)
    lc_t[...] = jnp.concatenate([log_cum] * 8, axis=0).T
    om_t[...] = jnp.concatenate([gap] * 8, axis=0).T

    def build_transfer(radial, scale):
        row = lc_ref[pl.ds(radial, 1), :]
        lanes = lax.broadcasted_iota(jnp.int32, (SLOTS, LANES), 1)

        def body(block, carry):
            rows = pl.ds(pl.multiple_of(block * SLOTS, SLOTS), SLOTS)
            pick = lanes == radial
            lc_col = jnp.sum(jnp.where(pick, lc_t[rows, :], 0.0), axis=1, keepdims=True)
            om_col = jnp.sum(jnp.where(pick, om_t[rows, :], 0.0), axis=1, keepdims=True)
            source = block * SLOTS + lax.broadcasted_iota(jnp.int32, (SLOTS, CELLS), 0)
            cell = lax.broadcasted_iota(jnp.int32, (SLOTS, CELLS), 1)
            value = jnp.where(
                source <= cell, (om_col * scale) * jnp.exp(jnp.minimum(row - lc_col, 0.0)), 0.0
            )
            high, low = split(value)
            tcat[rows, :] = high
            tcat[pl.ds(pl.multiple_of(CELLS + block * SLOTS, SLOTS), SLOTS), :] = low
            tcat[pl.ds(pl.multiple_of(2 * CELLS + block * SLOTS, SLOTS), SLOTS), :] = high
            return carry

        lax.fori_loop(0, CELLS // SLOTS, body, 0)

    build_transfer(az, section_factor)

    pltpu.make_async_copy(mode_buf.at[pl.ds(0, NAZ - 1)], mode_buf.at[pl.ds(0, NAZ - 1)], m_recv).wait()
    first_lanes = lax.broadcasted_iota(jnp.int32, (8, LANES), 1) < SLOTS
    mode_lane = [
        jnp.where(first_lanes, mode_buf[2 * q], mode_buf[2 * q + 1]) for q in range(4)
    ]
    for q in range(4):
        wide = jnp.concatenate([mode_lane[q].astype(F32)] * 16, axis=0)
        mode_sub[pl.ds(q * LANES, LANES), :] = wide.T
    mode_row = jnp.concatenate(mode_lane, axis=1)[0:1, :]

    def tables(block, carry):
        rows = pl.ds(pl.multiple_of(block * 16, 16), 16)
        point = block * 16 + lax.broadcasted_iota(jnp.int32, (16, HALF), 0)
        cos_value, sin_value = cos_sin((mode_row * point) & (M - 1))
        for table, value in ((cos_f, cos_value), (sin_f, sin_value)):
            high, low = split(value)
            table[rows, 0:HALF] = high
            table[rows, HALF : 2 * HALF] = high
            table[rows, 2 * HALF : 3 * HALF] = low
        mode_col = mode_sub[rows, :].astype(jnp.int32)
        for q in range(4):
            lane_point = q * LANES + lax.broadcasted_iota(jnp.int32, (16, LANES), 1)
            cos_value, sin_value = cos_sin((mode_col * lane_point) & (M - 1))
            cos_value = jnp.where(lane_point == 0, 0.5 * cos_value, cos_value)
            for table, value in ((cos_r, cos_value), (sin_r, sin_value)):
                high, low = split(value)
                table[rows, q * LANES : (q + 1) * LANES] = high
                table[rows, HALF + q * LANES : HALF + (q + 1) * LANES] = high
                table[rows, 2 * HALF + q * LANES : 2 * HALF + (q + 1) * LANES] = low
        return carry

    lax.fori_loop(0, HALF // 16, tables, 0)

    def self_mode(block, carry):
        modes = mode_sub[pl.ds(pl.multiple_of(block * 8, 8), 8), :]
        return carry + modes * is_self(modes)

    first_self = jnp.sum(
        lax.fori_loop(0, HALF // 8, self_mode, jnp.zeros((8, LANES), F32)), axis=0, keepdims=True
    )
    second_is_half = first_self == 0.0
    norm = 1.0 / math.sqrt(M)

    def second_cos(rows, start):
        point = start + lax.broadcasted_iota(jnp.int32, (rows, LANES), 0)
        return jnp.where(second_is_half & ((point & 1) == 1), -norm, norm)

    def put_rhs(buf, block, lanes, value):
        high, low = split(value)
        start = block * SLOTS
        buf[pl.ds(pl.multiple_of(start, SLOTS), SLOTS), lanes] = high
        buf[pl.ds(pl.multiple_of(HALF + start, SLOTS), SLOTS), lanes] = low
        buf[pl.ds(pl.multiple_of(2 * HALF + start, SLOTS), SLOTS), lanes] = high

    lane64 = lax.broadcasted_iota(jnp.int32, (SLOTS, LANES), 1)
    lane8 = lax.broadcasted_iota(jnp.int32, (8, LANES), 1)
    own_copy.wait()
    pltpu.make_async_copy(alone_send.at[pl.ds(0, NAZ - 1)], alone_recv.at[pl.ds(0, NAZ - 1)], a_recv).wait()

    def add_alone(source, total):
        return total + alone_recv[source]

    for half in range(2):
        alone_sum[half] = lax.fori_loop(
            half * (NAZ // 2), (half + 1) * (NAZ // 2), add_alone, jnp.zeros((8, LANES), F32)
        )

    def halo_copy(side):
        return pltpu.make_async_remote_copy(
            src_ref=halo_send.at[side], dst_ref=halo_recv.at[side],
            send_sem=h_send.at[side], recv_sem=h_recv.at[side],
            device_id=(ax_target(1 if side == 0 else NAX - 1), az), device_id_type=MESH,
        )

    def send_edges():
        def edges(block, carry):
            rows = pl.ds(pl.multiple_of(block * SLOTS, SLOTS), SLOTS)
            for side, lane in ((0, LANES - 1), (1, 0)):
                tile = jnp.zeros((SLOTS, LANES), F32)
                for c in range(4):
                    tile = jnp.where(lane64 == c, fp[0, c, rows, lane : lane + 1], tile)
                    tile = jnp.where(lane64 == 4 + c, fm[0, c, rows, lane : lane + 1], tile)
                halo_send[side, rows, :] = tile
            return carry

        lax.fori_loop(0, HALF // SLOTS, edges, 0)
        for side, lane in ((0, LANES - 1), (1, 0)):
            tile = jnp.zeros((8, LANES), F32)
            for c in range(4):
                tile = jnp.where(lane8 == c, fmid[0, c, :, lane : lane + 1], tile)
            halo_send[side, pl.ds(HALF, 8), :] = tile
        halo_copy(0).start()
        halo_copy(1).start()

    def forward(unit, carry):
        chunk = lax.div(unit, 2)
        pair = lax.rem(unit, 2)
        arrived = x_buf.at[chunk, pair, :, :, pl.ds(0, 7 * SLOTS), :]
        pltpu.make_async_copy(arrived, arrived, f_recv.at[unit]).wait()

        def fold(block, sums):
            rows = pl.ds(pl.multiple_of(block * SLOTS, SLOTS), SLOTS)
            modes = mode_sub[rows, :]
            double = 2.0 - 2.0 * is_self(modes)
            parity = jnp.where((modes.astype(jnp.int32) & 1) == 1, -norm, norm)
            out = []
            for place in range(2):
                even = double * x_buf[chunk, pair, place, 0, rows, :]
                odd = 2.0 * x_buf[chunk, pair, place, 1, rows, :]
                put_rhs(rhs_a, block, pl.ds(place * LANES, LANES), even)
                put_rhs(rhs_b, block, pl.ds(place * LANES, LANES), odd)
                out.append(sums[place] + fold_rows(parity * even))
            return tuple(out)

        zero = jnp.zeros((8, LANES), F32)
        sums = lax.fori_loop(0, HALF // SLOTS, fold, (zero,) * 2)
        first_rows = [alone_sum[0, pl.ds(4 * chunk + pair + 2 * place, 1), :] for place in range(2)]
        second_rows = [alone_sum[1, pl.ds(4 * chunk + pair + 2 * place, 1), :] for place in range(2)]
        for place in range(2):
            middle = jnp.sum(sums[place], axis=0, keepdims=True)
            middle = middle + (first_rows[place] + second_rows[place]) * norm
            fmid[chunk, pair + 2 * place] = jnp.broadcast_to(middle, (8, LANES))
        cos_sum = jnp.dot(cos_f[...], rhs_a[:, 0:CELLS], preferred_element_type=F32)
        sin_sum = jnp.dot(sin_f[...], rhs_b[:, 0:CELLS], preferred_element_type=F32)
        for c in range(2):
            lanes = slice(c * LANES, (c + 1) * LANES)
            fp[chunk, pair + 2 * c] = cos_sum[:, lanes]
            fm[chunk, pair + 2 * c] = sin_sum[:, lanes]

        def combine(block, carry):
            rows = pl.ds(pl.multiple_of(block * SLOTS, SLOTS), SLOTS)
            point = block * SLOTS + lax.broadcasted_iota(jnp.int32, (SLOTS, LANES), 0)
            first = jnp.where((~second_is_half) & ((point & 1) == 1), -norm, norm)
            second = jnp.where(second_is_half & ((point & 1) == 1), -norm, norm)
            for c in range(2):
                even = fp[chunk, pair + 2 * c, rows, :] + first * first_rows[c]
                even = even + second * second_rows[c]
                odd = fm[chunk, pair + 2 * c, rows, :]
                fp[chunk, pair + 2 * c, rows, :] = even - odd
                fm[chunk, pair + 2 * c, rows, :] = even + odd
            return carry

        lax.fori_loop(0, HALF // SLOTS, combine, 0)

        @pl.when(unit == 1)
        def _():
            send_edges()

        return carry

    lax.fori_loop(0, 3, forward, 0)
    halo_copy(0).wait()
    halo_copy(1).wait()
    left_on = jnp.where(ax > 0, 1.0, 0.0)
    right_on = jnp.where(ax < NAX - 1, 1.0, 0.0)
    here = inverse_radius(az)
    here_square = here * here

    def flux_pair(get, rows, c, left_lane0, left_lanec, cell):
        def cells(field):
            outer, inner = get(0, field), get(1, field)
            low_lanes = (lane64 if rows is not None else lane8) < LANES // 2
            return jnp.concatenate(
                [jnp.where(low_lanes, outer, inner), jnp.where(low_lanes, inner, outer)], axis=1
            )

        first, this, third = cells(0), cells(c), cells(2)
        axial = first * this
        after = pltpu.roll(axial, CELLS - 1, axis=1)
        before = pltpu.roll(axial, 1, axis=1)
        left, right = left_lane0, left_lanec
        before = jnp.where(cell == 0, left, before)
        after = jnp.where(cell == CELLS - 1, right, after)
        return (before - after) * 0.5, third * this

    def pick_lane(tile, lanes, index):
        return jnp.sum(jnp.where(lanes == index, tile, 0.0), axis=1, keepdims=True)

    def own_back(c):
        return pltpu.make_async_copy(
            e_send.at[c, :, :, pl.ds(lax.rem(az, 8) * SLOTS, SLOTS), :],
            e_recv.at[c, :, az],
            own_e.at[c],
        )

    def explicit(turn, carry):
        c = lax.rem(turn, 2) * 2 + lax.div(turn, 2)

        @pl.when(turn == 2)
        def _():
            forward(3, 0)

        def fluxes(block, sums):
            rows = pl.ds(pl.multiple_of(block * SLOTS, SLOTS), SLOTS)
            cell = lax.broadcasted_iota(jnp.int32, (SLOTS, CELLS), 1)
            tile_l = halo_recv[0, rows, :]
            tile_r = halo_recv[1, rows, :]
            both = []
            for shift, source in ((0, fp), (4, fm)):
                left = tile_l[:, shift : shift + 1] * pick_lane(tile_l, lane64, c + shift) * left_on
                right = tile_r[:, shift : shift + 1] * pick_lane(tile_r, lane64, c + shift) * right_on
                both.append(
                    flux_pair(
                        lambda chunk, field, source=source: source[chunk, field, rows, :],
                        rows, c, left, right, cell,
                    )
                )
            (div_p, azi_p), (div_m, azi_m) = both
            div_even = div_p + div_m
            put_rhs(rhs_a, block, pl.ds(0, CELLS), div_even)
            put_rhs(rhs_a, block, pl.ds(CELLS, CELLS), azi_p + azi_m)
            put_rhs(rhs_b, block, pl.ds(0, CELLS), div_p - div_m)
            put_rhs(rhs_b, block, pl.ds(CELLS, CELLS), azi_p - azi_m)
            second = second_cos(SLOTS, block * SLOTS)
            point = block * SLOTS + lax.broadcasted_iota(jnp.int32, (SLOTS, LANES), 0)
            second = jnp.where(point == 0, 0.5 * second, second)
            second = jnp.concatenate([second, second], axis=1)
            return sums + fold_rows(second * div_even)

        second_sum = lax.fori_loop(0, HALF // SLOTS, fluxes, jnp.zeros((8, CELLS), F32))
        tile_l = halo_recv[0, pl.ds(HALF, 8), :]
        tile_r = halo_recv[1, pl.ds(HALF, 8), :]
        cell = lax.broadcasted_iota(jnp.int32, (8, CELLS), 1)
        div_mid, azi_mid = flux_pair(
            lambda chunk, field: fmid[chunk, field], None, c,
            tile_l[:, 0:1] * pick_lane(tile_l, lane8, c) * left_on,
            tile_r[:, 0:1] * pick_lane(tile_r, lane8, c) * right_on,
            cell,
        )
        div_mid = div_mid[0:1, :]
        azi_mid = azi_mid[0:1, :]
        second_row = jnp.sum(second_sum, axis=0, keepdims=True) + div_mid * norm

        for half in range(2):
            lanes = slice(half * CELLS, (half + 1) * CELLS)
            e_raw[half] = jnp.dot(cos_r[...], rhs_a[:, lanes], preferred_element_type=F32)
            e_raw[2 + half] = jnp.dot(sin_r[...], rhs_b[:, lanes], preferred_element_type=F32)

        def finish(block, carry):
            rows = pl.ds(pl.multiple_of(block * SLOTS, SLOTS), SLOTS)
            modes = mode_sub[rows, :]
            parity = jnp.where((modes.astype(jnp.int32) & 1) == 1, -norm, norm)
            wave = signed(modes) * here_square
            alone = is_self(modes)
            parity, wave, alone = (jnp.concatenate([v, v], axis=1) for v in (parity, wave, alone))
            cos_div = e_raw[0, rows, :] + parity * div_mid
            cos_azi = e_raw[1, rows, :] + parity * azi_mid
            real = cos_div - wave * e_raw[3, rows, :]
            imag = alone * second_row - e_raw[2, rows, :] - wave * cos_azi
            for part, value in ((0, real), (1, imag)):
                high, low = split(value)
                where = pl.ds(pl.multiple_of(part * HALF + block * SLOTS, SLOTS), SLOTS)
                lhs_cat[where, 0:CELLS] = high
                lhs_cat[where, CELLS : 2 * CELLS] = high
                lhs_cat[where, 2 * CELLS : 3 * CELLS] = low
            return carry

        lax.fori_loop(0, HALF // SLOTS, finish, 0)
        for part in range(2):
            swept = jnp.dot(
                lhs_cat[part * HALF : (part + 1) * HALF, :], tcat[...], preferred_element_type=F32
            )
            for tile in range(2):
                e_send[c, tile, part] = swept[:, tile * LANES : (tile + 1) * LANES]
        own_back(c).start()

        def send_piece_back(piece, carry):
            tile = 1 - lax.div(piece, 2)
            part = lax.rem(piece, 2)

            def send_back(offset, carry):
                target = az_target(offset)
                pltpu.make_async_remote_copy(
                    src_ref=e_send.at[c, tile, part, pl.ds(lax.rem(target, 8) * SLOTS, SLOTS), :],
                    dst_ref=e_recv.at[c, tile, az, part],
                    send_sem=e_send_sem, recv_sem=e_recv_sem.at[2 * c + tile],
                    device_id=(ax, target), device_id_type=MESH,
                ).start()
                return carry

            return lax.fori_loop(1, NAZ, send_back, carry)

        lax.fori_loop(0, 4, send_piece_back, 0)
        return carry

    lax.fori_loop(0, FIELDS, explicit, 0)

    def state_sweep(radial, carry):
        build_transfer(radial, 1.0)
        there = inverse_radius(radial)
        ratio = signed(own_sub[...]) * there
        keep = 1.0 - (section_factor * viscosity) * ratio * ratio
        keep = jnp.concatenate([keep, keep], axis=1)
        for c in range(FIELDS):
            for part in range(2):
                high, low = split(st[radial, c, part] * keep)
                rows = pl.ds((2 * c + part) * SLOTS, SLOTS)
                lhs_cat[rows, 0:CELLS] = high
                lhs_cat[rows, CELLS : 2 * CELLS] = high
                lhs_cat[rows, 2 * CELLS : 3 * CELLS] = low
        swept = jnp.dot(lhs_cat[0:HALF, :], tcat[...], preferred_element_type=F32)
        st[radial] = swept.reshape(FIELDS, 2, SLOTS, CELLS)
        return carry

    lax.fori_loop(0, NR, state_sweep, 0)

    low_half = jnp.where(z < 2, 1.0, 0.0)
    swap = own_alone * (1.0 - low_half)
    flip = (1.0 - own_alone) * (2.0 * low_half - 1.0)
    decay_row = jnp.exp(lc_t[pl.ds(CELLS - 8, 8), :])[7:8, :]
    rel_buf[ax, pl.ds(SLOTS, 8), :] = jnp.broadcast_to(decay_row, (8, LANES))

    def send_last(offset, carry):
        pltpu.make_async_remote_copy(
            src_ref=rel_buf.at[ax], dst_ref=rel_buf.at[ax], send_sem=rel_send, recv_sem=rel_recv,
            device_id=(ax_target(offset), az), device_id_type=MESH,
        ).start()
        return carry

    def arrive(turn, last):
        c = lax.rem(turn, 2) * 2 + lax.div(turn, 2)
        own_back(c).wait()

        def add(tile, radial):
            lanes = pl.ds(tile * LANES, LANES)
            real = e_recv[c, tile, radial, 0]
            imag = e_recv[c, tile, radial, 1]
            new_real = st[radial, c, 0, :, lanes] + real + swap * (imag - real)
            new_imag = st[radial, c, 1, :, lanes] + flip * imag
            st[radial, c, 0, :, lanes] = new_real
            st[radial, c, 1, :, lanes] = new_imag
            return new_real, new_imag

        def landed(tile):
            ref = e_recv.at[c, tile, pl.ds(0, NAZ - 1)]
            pltpu.make_async_copy(ref, ref, e_recv_sem.at[2 * c + tile]).wait()

        def add_last(radial, last):
            new_real, new_imag = add(1, radial)
            where = c * 2 * NR + radial
            last = jnp.where(lane64 == where, new_real[:, LANES - 1 : LANES], last)
            return jnp.where(lane64 == where + NR, new_imag[:, LANES - 1 : LANES], last)

        def add_first(radial, carry):
            add(0, radial)
            pltpu.make_async_copy(st.at[radial, c], acc_ref.at[c, :, radial], out_sem.at[c]).start()
            return carry

        landed(1)
        last = lax.fori_loop(0, NR, add_last, last)

        @pl.when(c == FIELDS - 1)
        def _():
            rel_buf[ax, pl.ds(0, SLOTS), :] = last
            lax.fori_loop(1, NAX, send_last, 0)

        landed(0)
        lax.fori_loop(0, NR, add_first, 0)
        return last

    lax.fori_loop(0, FIELDS, arrive, jnp.zeros((SLOTS, LANES), F32))

    others = rel_buf.at[pl.ds(0, NAX - 1)]
    pltpu.make_async_copy(others, others, rel_recv).wait()

    def relay(block, incoming):
        upstream = rel_buf[block, pl.ds(0, SLOTS), :]
        decay = rel_buf[block, pl.ds(SLOTS, 8), :][0:1, :]
        return jnp.where(block < ax, decay * incoming + upstream, incoming)

    inflow = inflow_ref[...]
    inflow = jnp.concatenate([inflow, inflow], axis=1).T[:SLOTS, :]
    incoming = lax.fori_loop(0, NAX - 1, relay, inflow)
    incoming_ref[...] = jnp.concatenate([incoming, incoming], axis=0).T[:, :SLOTS]

    pltpu.make_async_copy(others, others, rel_send).wait()
    pltpu.make_async_copy(
        mode_buf.at[pl.ds(0, NAZ - 1)], mode_buf.at[pl.ds(0, NAZ - 1)], m_send
    ).wait()
    alone_sent = alone_recv.at[pl.ds(0, NAZ - 1)]
    pltpu.make_async_copy(alone_sent, alone_sent, a_send).wait()
    sent = x_buf.at[:, :, :, :, pl.ds(0, 7 * SLOTS), :]
    pltpu.make_async_copy(sent, sent, f_send).wait()
    sent_back = e_recv.at[:, :, pl.ds(0, NAZ - 1)]
    pltpu.make_async_copy(sent_back, sent_back, e_send_sem).wait()

    def written(c, carry):
        pltpu.make_async_copy(acc_ref.at[c], acc_ref.at[c], out_sem.at[c]).wait()
        return carry

    lax.fori_loop(0, FIELDS, written, 0)


def shards(state, inflow, courant, mode_number, partner_table):
    modes = mode_number.reshape(1, SLOTS)
    inflow_rows = inflow.reshape(FIELDS * 2 * NR, SLOTS)
    dma = pltpu.SemaphoreType.DMA
    vmem = pltpu.VMEM
    acc, incoming, reach = pl.pallas_call(
        kernel,
        out_shape=(
            jax.ShapeDtypeStruct((FIELDS, 2, NR, SLOTS, CELLS), F32),
            jax.ShapeDtypeStruct((FIELDS * 2 * NR, SLOTS), F32),
            jax.ShapeDtypeStruct((NR, CELLS), F32),
        ),
        in_specs=[
            pl.BlockSpec(memory_space=pl.ANY),
            pl.BlockSpec(memory_space=pltpu.VMEM),
            pl.BlockSpec(memory_space=pltpu.VMEM),
            pl.BlockSpec(memory_space=pltpu.VMEM),
        ],
        out_specs=(
            pl.BlockSpec(memory_space=pl.ANY),
            pl.BlockSpec(memory_space=pltpu.VMEM),
            pl.BlockSpec(memory_space=pltpu.VMEM),
        ),
        scratch_shapes=[
            vmem((NR, FIELDS, 2, SLOTS, CELLS), F32),
            vmem((NAZ, 2, 2, 2, 2, SLOTS, LANES), F32),
            vmem((2, 2, 2, 2, HALF, LANES), F32),
            vmem((NAZ, 8, LANES), F32),
            vmem((NAZ, 8, LANES), F32),
            vmem((2, 8, LANES), F32),
            vmem((NAZ, 8, LANES), jnp.int32),
            vmem((HALF, LANES), F32),
            vmem((SLOTS, LANES), F32),
            vmem((HALF, 3 * HALF), BF16),
            vmem((HALF, 3 * HALF), BF16),
            vmem((HALF, 3 * HALF), BF16),
            vmem((HALF, 3 * HALF), BF16),
            vmem((3 * HALF, 4 * LANES), BF16),
            vmem((3 * HALF, 4 * LANES), BF16),
            vmem((3 * CELLS, CELLS), BF16),
            vmem((2, FIELDS, HALF, LANES), F32),
            vmem((2, FIELDS, HALF, LANES), F32),
            vmem((2, FIELDS, 8, LANES), F32),
            vmem((2, HALF + 8, LANES), F32),
            vmem((2, HALF + 8, LANES), F32),
            vmem((NR, CELLS), F32),
            vmem((CELLS, LANES), F32),
            vmem((CELLS, LANES), F32),
            vmem((4, HALF, CELLS), F32),
            vmem((FIELDS, 2, 2, HALF, LANES), F32),
            vmem((FIELDS, 2, NAZ, 2, SLOTS, LANES), F32),
            vmem((M, 3 * CELLS), BF16),
            vmem((NAX, SLOTS + 8, LANES), F32),
            dma((NAZ,)),
            dma,
            dma((4,)),
            dma,
            dma,
            dma,
            dma,
            dma,
            dma((2,)),
            dma((2,)),
            dma,
            dma((2 * FIELDS,)),
            dma((FIELDS,)),
            dma((FIELDS,)),
            dma,
            dma,
        ],
        compiler_params=pltpu.CompilerParams(
            collective_id=0, has_side_effects=True, vmem_limit_bytes=58 * 2**20
        ),
    )(state, courant, modes, inflow_rows)
    incoming_full = incoming.reshape(FIELDS, 2, NR, SLOTS)
    return acc + reach[None, None, :, None, :] * incoming_full[..., None]


def solution(mesh):
    in_specs = (
        P(None, None, None, "az", "ax"),
        P(None, None, None, "az"),
        P(None, "ax"),
        P("az"),
        P("az"),
    )
    out_specs = P(None, None, None, "az", "ax")
    return jax.shard_map(shards, mesh=mesh, in_specs=in_specs, out_specs=out_specs, check_vma=False)
```

```python
import functools
import math

import jax
import jax.numpy as jnp
from jax import lax
from jax.experimental import pallas as pl
from jax.experimental.pallas import tpu as pltpu
from jax.sharding import PartitionSpec as P

section_factor = 0.5
viscosity = 0.02
M = 1024
HALF = M // 2
FIELDS = 4
NR = 16
SLOTS = 64
CELLS = 256
NAZ = 16
NAX = 8
LANES = 128
MESH = pl.DeviceIdType.MESH
F32 = jnp.float32
BF16 = jnp.bfloat16


def split(value):
    high = value.astype(BF16)
    low = (value - high.astype(F32)).astype(BF16)
    return high, low


def inverse_radius(radial_id):
    ratio = (0.6 + 0.4 * (radial_id.astype(F32) + 0.5) / NR) * (M / (2.0 * math.pi))
    return 1.0 / ratio


def cos_sin(phase):
    quadrant = lax.shift_right_logical(phase + 128, 8)
    angle = (phase - quadrant * 256).astype(F32) * (2.0 * math.pi / M)
    square = angle * angle
    sine = angle * (
        1.0
        + square
        * (-1.0 / 6 + square * (1.0 / 120 + square * (-1.0 / 5040 + square * (1.0 / 362880))))
    )
    cosine = 1.0 + square * (
        -0.5 + square * (1.0 / 24 + square * (-1.0 / 720 + square * (1.0 / 40320)))
    )
    odd = (quadrant & 1) == 1
    norm = 1.0 / math.sqrt(M)
    cos_value = jnp.where(odd, sine, cosine)
    sin_value = jnp.where(odd, cosine, sine)
    cos_sign = jnp.where(((quadrant + 1) & 2) == 2, -norm, norm)
    sin_sign = jnp.where((quadrant & 2) == 2, -norm, norm)
    return cos_value * cos_sign, sin_value * sin_sign


def signed(modes):
    return jnp.where(modes < HALF, modes, jnp.where(modes == HALF, 0.0, modes - M))


def is_self(modes):
    return jnp.where((modes == 0.0) | (modes == float(HALF)), 1.0, 0.0)


def fold_rows(value):
    rows, lanes = value.shape
    return jnp.sum(value.reshape(rows // 8, 8, lanes), axis=0)


def kernel(
    state_ref, courant_ref, mode_ref, inflow_ref,
    acc_ref, incoming_ref, reach_ref,
    st, send_buf, x_buf, alone_send, alone_recv, alone_sum, mode_buf, mode_sub, own_sub,
    cos_f, sin_f, cos_r, sin_r, rhs_a, rhs_b, tcat,
    fp, fm, fmid, halo_send, halo_recv,
    lc_ref, lc_t, om_t, e_raw, e_send, e_recv, lhs_cat, rel_buf,
    st_sem, f_send, f_recv, a_send, a_recv, m_send, m_recv, own_x, h_send, h_recv,
    e_send_sem, e_recv_sem, own_e, out_sem, rel_send, rel_recv,
):
    ax = lax.axis_index("ax")
    az = lax.axis_index("az")
    z = lax.div(az, 4)
    y = lax.rem(az, 4)

    def az_target(offset):
        step = lax.rem(offset * 7, NAZ)
        return lax.rem(z + lax.div(step, 4), 4) * 4 + lax.rem(y + lax.rem(step, 4), 4)

    def ax_target(offset):
        return lax.rem(ax + offset, NAX)

    def start_state(offset, carry):
        turn = lax.div(offset, 4)
        step = lax.rem(1 + 2 * turn + lax.div(turn, 2) * 3, 4)
        target = lax.rem(z + step, 4) * 4 + lax.rem(y + lax.rem(offset, 4), 4)
        pltpu.make_async_copy(
            state_ref.at[:, :, target], st.at[target], st_sem.at[target]
        ).start()
        return carry

    lax.fori_loop(0, NAZ, start_state, 0)

    barrier = pltpu.get_barrier_semaphore()

    def greet_az(offset, carry):
        pl.semaphore_signal(barrier, inc=1, device_id=(ax, az_target(offset)), device_id_type=MESH)
        return carry

    def greet_ax(offset, carry):
        pl.semaphore_signal(barrier, inc=1, device_id=(ax_target(offset), az), device_id_type=MESH)
        return carry

    lax.fori_loop(1, NAZ, greet_az, 0)
    lax.fori_loop(1, NAX, greet_ax, 0)

    modes_here = mode_ref[...]
    mode_buf[az] = jnp.broadcast_to(jnp.concatenate([modes_here, modes_here], axis=1), (8, LANES))

    own_sub[...] = jnp.concatenate([mode_buf[az].astype(F32)] * 16, axis=0).T[:SLOTS, :]

    group = lax.rem(z, 2) * 4 + y
    sign = jnp.where(z < 2, 1.0, -1.0)
    low_lanes = lax.broadcasted_iota(jnp.int32, (SLOTS, LANES), 1) < LANES // 2

    def column(step, dy):
        return lax.rem(z + step, 4) * 4 + lax.rem(y + dy, 4)

    def state_here(target):
        pltpu.make_async_copy(
            state_ref.at[:, :, target], st.at[target], st_sem.at[target]
        ).wait()

    def pack(step, parts):
        def body(dy, carry):
            target = column(step, dy)
            state_here(target)
            for field in range(FIELDS):
                for part in parts:
                    first = st[target, field, part, :, 0:LANES]
                    second = st[target, field, part, :, LANES:CELLS]
                    if part == 1:
                        first, second = first * sign, second * sign
                    pair, place = field % 2, field // 2
                    send_buf[target, 0, pair, place, part] = jnp.where(low_lanes, first, second)
                    send_buf[target, 1, pair, place, part] = jnp.where(low_lanes, second, first)
            return carry

        lax.fori_loop(0, 4, body, 0)

    pack(1, (0,))
    pack(3, (1,))
    pl.semaphore_wait(barrier, NAZ - 1 + NAX - 1)

    def send_modes(offset, carry):
        pltpu.make_async_remote_copy(
            src_ref=mode_buf.at[az], dst_ref=mode_buf.at[az], send_sem=m_send, recv_sem=m_recv,
            device_id=(ax, az_target(offset)), device_id_type=MESH,
        ).start()
        return carry

    lax.fori_loop(1, NAZ, send_modes, 0)

    def send_piece(chunk, pair, place, index):
        same = lax.div(index, 8)
        part = (1 - same) * lax.div(index, 4) + same * lax.rem(index, 2)
        step = (1 - same) * (1 + 2 * lax.div(index, 4))
        dy = (1 - same) * lax.rem(index, 4) + same * (lax.div(index, 2) - 3)
        target = column(step, dy)
        pltpu.make_async_remote_copy(
            src_ref=send_buf.at[target, chunk, pair, place, part],
            dst_ref=x_buf.at[chunk, pair, place, part, pl.ds(group * SLOTS, SLOTS), :],
            send_sem=f_send, recv_sem=f_recv.at[2 * pair + chunk],
            device_id=(ax, target), device_id_type=MESH,
        ).start()

    def send_first(index, carry):
        send_piece(0, 0, 0, index)
        return carry

    lax.fori_loop(0, 8, send_first, 0)
    pack(0, (0, 1))
    lax.fori_loop(8, 14, send_first, 0)

    def send_rest(piece, carry):
        def send_more(count, carry):
            send_piece(
                lax.rem(lax.div(piece, 2), 2), lax.div(piece, 4), lax.rem(piece, 2),
                lax.rem(count * 5, 14),
            )
            return carry

        return lax.fori_loop(0, 14, send_more, carry)

    lax.fori_loop(1, 2, send_rest, 0)

    own_alone = is_self(own_sub[...])

    def alone_there(dy, carry):
        state_here(column(2, dy))
        return carry

    lax.fori_loop(0, 4, alone_there, 0)

    def alone_row(radial, carry):
        rows = [[], []]
        for field in range(FIELDS):
            first = jnp.sum(own_alone * st[radial, field, 0, :, 0:LANES], axis=0, keepdims=True)
            second = jnp.sum(own_alone * st[radial, field, 0, :, LANES:CELLS], axis=0, keepdims=True)
            rows[0].append(jnp.where(low_lanes[0:1], first, second))
            rows[1].append(jnp.where(low_lanes[0:1], second, first))
        alone_send[radial] = jnp.concatenate(rows[0] + rows[1], axis=0)
        return carry

    lax.fori_loop(0, NR, alone_row, 0)
    alone_recv[az] = alone_send[az]

    def send_alone(offset, carry):
        target = az_target(offset)
        pltpu.make_async_remote_copy(
            src_ref=alone_send.at[target], dst_ref=alone_recv.at[az], send_sem=a_send,
            recv_sem=a_recv, device_id=(ax, target), device_id_type=MESH,
        ).start()
        return carry

    lax.fori_loop(1, NAZ, send_alone, 0)
    lax.fori_loop(2, 8, send_rest, 0)

    own_copy = pltpu.make_async_copy(
        send_buf.at[az], x_buf.at[:, :, :, :, pl.ds(group * SLOTS, SLOTS), :], own_x
    )
    own_copy.start()

    courant = courant_ref[...]
    weight = courant / (1.0 + courant)
    gap = 1.0 - weight
    series = gap * (
        1.0 + gap * (1.0 / 2 + gap * (1.0 / 3 + gap * (1.0 / 4 + gap * (1.0 / 5 + gap * (1.0 / 6)))))
    )
    log_weight = jnp.where(gap < 0.05, -series, jnp.log(weight))
    row_ids = lax.broadcasted_iota(jnp.int32, (CELLS, CELLS), 0)
    col_ids = lax.broadcasted_iota(jnp.int32, (CELLS, CELLS), 1)
    upper = jnp.where(row_ids <= col_ids, 1.0, 0.0)
    log_cum = jnp.dot(
        log_weight, upper, preferred_element_type=F32, precision=lax.Precision.HIGHEST
    )
    lc_ref[...] = log_cum
    reach_ref[...] = jnp.exp(log_cum)
    lc_t[...] = jnp.concatenate([log_cum] * 8, axis=0).T
    om_t[...] = jnp.concatenate([gap] * 8, axis=0).T

    def build_transfer(radial, scale):
        row = lc_ref[pl.ds(radial, 1), :]
        lanes = lax.broadcasted_iota(jnp.int32, (SLOTS, LANES), 1)

        def body(block, carry):
            rows = pl.ds(pl.multiple_of(block * SLOTS, SLOTS), SLOTS)
            pick = lanes == radial
            lc_col = jnp.sum(jnp.where(pick, lc_t[rows, :], 0.0), axis=1, keepdims=True)
            om_col = jnp.sum(jnp.where(pick, om_t[rows, :], 0.0), axis=1, keepdims=True)
            source = block * SLOTS + lax.broadcasted_iota(jnp.int32, (SLOTS, CELLS), 0)
            cell = lax.broadcasted_iota(jnp.int32, (SLOTS, CELLS), 1)
            value = jnp.where(
                source <= cell, (om_col * scale) * jnp.exp(jnp.minimum(row - lc_col, 0.0)), 0.0
            )
            high, low = split(value)
            tcat[rows, :] = high
            tcat[pl.ds(pl.multiple_of(CELLS + block * SLOTS, SLOTS), SLOTS), :] = low
            tcat[pl.ds(pl.multiple_of(2 * CELLS + block * SLOTS, SLOTS), SLOTS), :] = high
            return carry

        lax.fori_loop(0, CELLS // SLOTS, body, 0)

    build_transfer(az, section_factor)

    pltpu.make_async_copy(mode_buf.at[pl.ds(0, NAZ - 1)], mode_buf.at[pl.ds(0, NAZ - 1)], m_recv).wait()
    first_lanes = lax.broadcasted_iota(jnp.int32, (8, LANES), 1) < SLOTS
    mode_lane = [
        jnp.where(first_lanes, mode_buf[2 * q], mode_buf[2 * q + 1]) for q in range(4)
    ]
    for q in range(4):
        wide = jnp.concatenate([mode_lane[q].astype(F32)] * 16, axis=0)
        mode_sub[pl.ds(q * LANES, LANES), :] = wide.T
    mode_row = jnp.concatenate(mode_lane, axis=1)[0:1, :]

    def tables(block, carry):
        rows = pl.ds(pl.multiple_of(block * 16, 16), 16)
        point = block * 16 + lax.broadcasted_iota(jnp.int32, (16, HALF), 0)
        cos_value, sin_value = cos_sin((mode_row * point) & (M - 1))
        for table, value in ((cos_f, cos_value), (sin_f, sin_value)):
            high, low = split(value)
            table[rows, 0:HALF] = high
            table[rows, HALF : 2 * HALF] = high
            table[rows, 2 * HALF : 3 * HALF] = low
        mode_col = mode_sub[rows, :].astype(jnp.int32)
        for q in range(4):
            lane_point = q * LANES + lax.broadcasted_iota(jnp.int32, (16, LANES), 1)
            cos_value, sin_value = cos_sin((mode_col * lane_point) & (M - 1))
            cos_value = jnp.where(lane_point == 0, 0.5 * cos_value, cos_value)
            for table, value in ((cos_r, cos_value), (sin_r, sin_value)):
                high, low = split(value)
                table[rows, q * LANES : (q + 1) * LANES] = high
                table[rows, HALF + q * LANES : HALF + (q + 1) * LANES] = high
                table[rows, 2 * HALF + q * LANES : 2 * HALF + (q + 1) * LANES] = low
        return carry

    lax.fori_loop(0, HALF // 16, tables, 0)

    def self_mode(block, carry):
        modes = mode_sub[pl.ds(pl.multiple_of(block * 8, 8), 8), :]
        return carry + modes * is_self(modes)

    first_self = jnp.sum(
        lax.fori_loop(0, HALF // 8, self_mode, jnp.zeros((8, LANES), F32)), axis=0, keepdims=True
    )
    second_is_half = first_self == 0.0
    norm = 1.0 / math.sqrt(M)

    def second_cos(rows, start):
        point = start + lax.broadcasted_iota(jnp.int32, (rows, LANES), 0)
        return jnp.where(second_is_half & ((point & 1) == 1), -norm, norm)

    def put_rhs(buf, block, lanes, value):
        high, low = split(value)
        start = block * SLOTS
        buf[pl.ds(pl.multiple_of(start, SLOTS), SLOTS), lanes] = high
        buf[pl.ds(pl.multiple_of(HALF + start, SLOTS), SLOTS), lanes] = low
        buf[pl.ds(pl.multiple_of(2 * HALF + start, SLOTS), SLOTS), lanes] = high

    lane64 = lax.broadcasted_iota(jnp.int32, (SLOTS, LANES), 1)
    lane8 = lax.broadcasted_iota(jnp.int32, (8, LANES), 1)
    own_copy.wait()
    pltpu.make_async_copy(alone_send.at[pl.ds(0, NAZ - 1)], alone_recv.at[pl.ds(0, NAZ - 1)], a_recv).wait()

    def add_alone(source, total):
        return total + alone_recv[source]

    for half in range(2):
        alone_sum[half] = lax.fori_loop(
            half * (NAZ // 2), (half + 1) * (NAZ // 2), add_alone, jnp.zeros((8, LANES), F32)
        )

    def halo_copy(pair, side):
        return pltpu.make_async_remote_copy(
            src_ref=halo_send.at[pair, side], dst_ref=halo_recv.at[pair, side],
            send_sem=h_send.at[2 * pair + side], recv_sem=h_recv.at[2 * pair + side],
            device_id=(ax_target(1 if side == 0 else NAX - 1), az), device_id_type=MESH,
        )

    def send_edges(pair):
        def edges(block, carry):
            rows = pl.ds(pl.multiple_of(block * SLOTS, SLOTS), SLOTS)
            for side, lane in ((0, LANES - 1), (1, 0)):
                tile = jnp.zeros((SLOTS, LANES), F32)
                for place in range(2):
                    field = pair + 2 * place
                    tile = jnp.where(lane64 == place, fp[0, field, rows, lane : lane + 1], tile)
                    tile = jnp.where(lane64 == 4 + place, fm[0, field, rows, lane : lane + 1], tile)
                halo_send[pair, side, rows, :] = tile
            return carry

        lax.fori_loop(0, HALF // SLOTS, edges, 0)
        for side, lane in ((0, LANES - 1), (1, 0)):
            tile = jnp.zeros((8, LANES), F32)
            for place in range(2):
                tile = jnp.where(
                    lane8 == place, fmid[0, pair + 2 * place, :, lane : lane + 1], tile
                )
            halo_send[pair, side, pl.ds(HALF, 8), :] = tile
        halo_copy(pair, 0).start()
        halo_copy(pair, 1).start()

    def forward(unit, carry):
        chunk = lax.rem(unit, 2)
        pair = lax.div(unit, 2)
        arrived = x_buf.at[chunk, pair, :, :, pl.ds(0, 7 * SLOTS), :]
        pltpu.make_async_copy(arrived, arrived, f_recv.at[unit]).wait()

        def fold(block, sums):
            rows = pl.ds(pl.multiple_of(block * SLOTS, SLOTS), SLOTS)
            modes = mode_sub[rows, :]
            double = 2.0 - 2.0 * is_self(modes)
            parity = jnp.where((modes.astype(jnp.int32) & 1) == 1, -norm, norm)
            out = []
            for place in range(2):
                even = double * x_buf[chunk, pair, place, 0, rows, :]
                odd = 2.0 * x_buf[chunk, pair, place, 1, rows, :]
                put_rhs(rhs_a, block, pl.ds(place * LANES, LANES), even)
                put_rhs(rhs_b, block, pl.ds(place * LANES, LANES), odd)
                out.append(sums[place] + fold_rows(parity * even))
            return tuple(out)

        zero = jnp.zeros((8, LANES), F32)
        sums = lax.fori_loop(0, HALF // SLOTS, fold, (zero,) * 2)
        first_rows = [alone_sum[0, pl.ds(4 * chunk + pair + 2 * place, 1), :] for place in range(2)]
        second_rows = [alone_sum[1, pl.ds(4 * chunk + pair + 2 * place, 1), :] for place in range(2)]
        for place in range(2):
            middle = jnp.sum(sums[place], axis=0, keepdims=True)
            middle = middle + (first_rows[place] + second_rows[place]) * norm
            fmid[chunk, pair + 2 * place] = jnp.broadcast_to(middle, (8, LANES))
        cos_sum = jnp.dot(cos_f[...], rhs_a[:, 0:CELLS], preferred_element_type=F32)
        sin_sum = jnp.dot(sin_f[...], rhs_b[:, 0:CELLS], preferred_element_type=F32)
        for c in range(2):
            lanes = slice(c * LANES, (c + 1) * LANES)
            fp[chunk, pair + 2 * c] = cos_sum[:, lanes]
            fm[chunk, pair + 2 * c] = sin_sum[:, lanes]

        def combine(block, carry):
            rows = pl.ds(pl.multiple_of(block * SLOTS, SLOTS), SLOTS)
            point = block * SLOTS + lax.broadcasted_iota(jnp.int32, (SLOTS, LANES), 0)
            first = jnp.where((~second_is_half) & ((point & 1) == 1), -norm, norm)
            second = jnp.where(second_is_half & ((point & 1) == 1), -norm, norm)
            for c in range(2):
                even = fp[chunk, pair + 2 * c, rows, :] + first * first_rows[c]
                even = even + second * second_rows[c]
                odd = fm[chunk, pair + 2 * c, rows, :]
                fp[chunk, pair + 2 * c, rows, :] = even - odd
                fm[chunk, pair + 2 * c, rows, :] = even + odd
            return carry

        lax.fori_loop(0, HALF // SLOTS, combine, 0)

        @pl.when(chunk == 0)
        def _():
            send_edges(pair)

        return carry

    lax.fori_loop(0, 2, forward, 0)
    halo_copy(0, 0).wait()
    halo_copy(0, 1).wait()
    left_on = jnp.where(ax > 0, 1.0, 0.0)
    right_on = jnp.where(ax < NAX - 1, 1.0, 0.0)
    here = inverse_radius(az)
    here_square = here * here

    def flux_pair(get, rows, c, left_lane0, left_lanec, cell):
        def cells(field):
            outer, inner = get(0, field), get(1, field)
            low_lanes = (lane64 if rows is not None else lane8) < LANES // 2
            return jnp.concatenate(
                [jnp.where(low_lanes, outer, inner), jnp.where(low_lanes, inner, outer)], axis=1
            )

        first, this, third = cells(0), cells(c), cells(2)
        axial = first * this
        after = pltpu.roll(axial, CELLS - 1, axis=1)
        before = pltpu.roll(axial, 1, axis=1)
        left, right = left_lane0, left_lanec
        before = jnp.where(cell == 0, left, before)
        after = jnp.where(cell == CELLS - 1, right, after)
        return (before - after) * 0.5, third * this

    def pick_lane(tile, lanes, index):
        return jnp.sum(jnp.where(lanes == index, tile, 0.0), axis=1, keepdims=True)

    def own_back(c):
        return pltpu.make_async_copy(
            e_send.at[c, :, :, pl.ds(lax.rem(az, 8) * SLOTS, SLOTS), :],
            e_recv.at[c, :, az],
            own_e.at[c],
        )

    def explicit(turn, carry):
        c = lax.rem(turn, 2) * 2 + lax.div(turn, 2)

        @pl.when(turn == 2)
        def _():
            lax.fori_loop(2, 4, forward, 0)
            halo_copy(1, 0).wait()
            halo_copy(1, 1).wait()

        def fluxes(block, sums):
            rows = pl.ds(pl.multiple_of(block * SLOTS, SLOTS), SLOTS)
            cell = lax.broadcasted_iota(jnp.int32, (SLOTS, CELLS), 1)
            tile_l = halo_recv[0, 0, rows, :]
            tile_r = halo_recv[0, 1, rows, :]
            this_l = halo_recv[lax.rem(c, 2), 0, rows, :]
            this_r = halo_recv[lax.rem(c, 2), 1, rows, :]
            place = lax.div(c, 2)
            both = []
            for shift, source in ((0, fp), (4, fm)):
                left = tile_l[:, shift : shift + 1] * pick_lane(this_l, lane64, place + shift) * left_on
                right = tile_r[:, shift : shift + 1] * pick_lane(this_r, lane64, place + shift) * right_on
                both.append(
                    flux_pair(
                        lambda chunk, field, source=source: source[chunk, field, rows, :],
                        rows, c, left, right, cell,
                    )
                )
            (div_p, azi_p), (div_m, azi_m) = both
            div_even = div_p + div_m
            put_rhs(rhs_a, block, pl.ds(0, CELLS), div_even)
            put_rhs(rhs_a, block, pl.ds(CELLS, CELLS), azi_p + azi_m)
            put_rhs(rhs_b, block, pl.ds(0, CELLS), div_p - div_m)
            put_rhs(rhs_b, block, pl.ds(CELLS, CELLS), azi_p - azi_m)
            second = second_cos(SLOTS, block * SLOTS)
            point = block * SLOTS + lax.broadcasted_iota(jnp.int32, (SLOTS, LANES), 0)
            second = jnp.where(point == 0, 0.5 * second, second)
            second = jnp.concatenate([second, second], axis=1)
            return sums + fold_rows(second * div_even)

        second_sum = lax.fori_loop(0, HALF // SLOTS, fluxes, jnp.zeros((8, CELLS), F32))
        tile_l = halo_recv[0, 0, pl.ds(HALF, 8), :]
        tile_r = halo_recv[0, 1, pl.ds(HALF, 8), :]
        this_l = halo_recv[lax.rem(c, 2), 0, pl.ds(HALF, 8), :]
        this_r = halo_recv[lax.rem(c, 2), 1, pl.ds(HALF, 8), :]
        place = lax.div(c, 2)
        cell = lax.broadcasted_iota(jnp.int32, (8, CELLS), 1)
        div_mid, azi_mid = flux_pair(
            lambda chunk, field: fmid[chunk, field], None, c,
            tile_l[:, 0:1] * pick_lane(this_l, lane8, place) * left_on,
            tile_r[:, 0:1] * pick_lane(this_r, lane8, place) * right_on,
            cell,
        )
        div_mid = div_mid[0:1, :]
        azi_mid = azi_mid[0:1, :]
        second_row = jnp.sum(second_sum, axis=0, keepdims=True) + div_mid * norm

        for half in range(2):
            lanes = slice(half * CELLS, (half + 1) * CELLS)
            e_raw[half] = jnp.dot(cos_r[...], rhs_a[:, lanes], preferred_element_type=F32)
            e_raw[2 + half] = jnp.dot(sin_r[...], rhs_b[:, lanes], preferred_element_type=F32)

        def finish(block, carry):
            rows = pl.ds(pl.multiple_of(block * SLOTS, SLOTS), SLOTS)
            modes = mode_sub[rows, :]
            parity = jnp.where((modes.astype(jnp.int32) & 1) == 1, -norm, norm)
            wave = signed(modes) * here_square
            alone = is_self(modes)
            parity, wave, alone = (jnp.concatenate([v, v], axis=1) for v in (parity, wave, alone))
            cos_div = e_raw[0, rows, :] + parity * div_mid
            cos_azi = e_raw[1, rows, :] + parity * azi_mid
            real = cos_div - wave * e_raw[3, rows, :]
            imag = alone * second_row - e_raw[2, rows, :] - wave * cos_azi
            for part, value in ((0, real), (1, imag)):
                high, low = split(value)
                where = pl.ds(pl.multiple_of(part * HALF + block * SLOTS, SLOTS), SLOTS)
                lhs_cat[where, 0:CELLS] = high
                lhs_cat[where, CELLS : 2 * CELLS] = high
                lhs_cat[where, 2 * CELLS : 3 * CELLS] = low
            return carry

        lax.fori_loop(0, HALF // SLOTS, finish, 0)
        for part in range(2):
            swept = jnp.dot(
                lhs_cat[part * HALF : (part + 1) * HALF, :], tcat[...], preferred_element_type=F32
            )
            for tile in range(2):
                e_send[c, tile, part] = swept[:, tile * LANES : (tile + 1) * LANES]
        own_back(c).start()
        return carry

    def field_of(turn):
        return lax.rem(turn, 2) * 2 + lax.div(turn, 2)

    def block_back(turn, tile, part, target, same):
        c = field_of(turn)
        pltpu.make_async_remote_copy(
            src_ref=e_send.at[c, tile, part, pl.ds(lax.rem(target, 8) * SLOTS, SLOTS), :],
            dst_ref=e_recv.at[c, tile, az, part],
            send_sem=e_send_sem, recv_sem=e_recv_sem.at[same, 2 * c + tile],
            device_id=(ax, target), device_id_type=MESH,
        ).start()

    def send_back(turn, tile):
        def part_body(part, carry):
            def body(count, carry):
                index = lax.rem(count * 5, 12)
                near = lax.div(index, 8)
                same = lax.div(index, 9)
                step = (1 - near) * (1 + 2 * lax.div(index, 4)) + (near - same) * 2
                dy = (1 - near) * lax.rem(index, 4) + near * (index - 8)
                block_back(turn, tile, part, column(step, dy), same)
                return carry

            return lax.fori_loop(0, 12, body, carry)

        lax.fori_loop(0, 2, part_body, 0)

    def send_back_direct(turn, tile):
        def part_body(part, carry):
            def body(offset, carry):
                target = az_target(offset)
                step = lax.rem(lax.div(target, 4) + 4 - z, 4)
                block_back(turn, tile, part, target, 1 - lax.div(step + 3, 4))
                return carry

            return lax.fori_loop(1, NAZ, body, carry)

        lax.fori_loop(0, 2, part_body, 0)

    def same_landed(turn, tile):
        c = field_of(turn)
        ref = e_recv.at[c, tile, pl.ds(0, 3)]
        pltpu.make_async_copy(ref, ref, e_recv_sem.at[1, 2 * c + tile]).wait()

    def forward_on(turn, tile):
        c = field_of(turn)
        same_landed(turn, tile)

        def body(count, carry):
            block = e_recv.at[c, tile, column(0, 1 + lax.div(count, 2)), lax.rem(count, 2)]
            pltpu.make_async_remote_copy(
                src_ref=block, dst_ref=block,
                send_sem=e_send_sem, recv_sem=e_recv_sem.at[0, 2 * c + tile],
                device_id=(ax, column(2, 0)), device_id_type=MESH,
            ).start()
            return carry

        lax.fori_loop(0, 6, body, 0)

    def work(turn, carry):
        explicit(turn, 0)

        @pl.when(turn >= 2)
        def _():
            forward_on(turn - 2, 1)
            forward_on(turn - 2, 0)

        @pl.when(turn < 2)
        def _():
            send_back(turn, 1)
            send_back(turn, 0)

        @pl.when(turn == 2)
        def _():
            send_back_direct(turn, 1)
            send_back_direct(turn, 0)

        return carry

    lax.fori_loop(0, FIELDS, work, 0)
    send_back_direct(FIELDS - 1, 1)

    def state_sweep(radial, carry):
        build_transfer(radial, 1.0)
        there = inverse_radius(radial)
        ratio = signed(own_sub[...]) * there
        keep = 1.0 - (section_factor * viscosity) * ratio * ratio
        keep = jnp.concatenate([keep, keep], axis=1)
        for c in range(FIELDS):
            for part in range(2):
                high, low = split(st[radial, c, part] * keep)
                rows = pl.ds((2 * c + part) * SLOTS, SLOTS)
                lhs_cat[rows, 0:CELLS] = high
                lhs_cat[rows, CELLS : 2 * CELLS] = high
                lhs_cat[rows, 2 * CELLS : 3 * CELLS] = low
        swept = jnp.dot(lhs_cat[0:HALF, :], tcat[...], preferred_element_type=F32)
        st[radial] = swept.reshape(FIELDS, 2, SLOTS, CELLS)
        return carry

    send_back_direct(FIELDS - 1, 0)
    lax.fori_loop(0, NR, state_sweep, 0)

    low_half = jnp.where(z < 2, 1.0, 0.0)
    swap = own_alone * (1.0 - low_half)
    flip = (1.0 - own_alone) * (2.0 * low_half - 1.0)
    decay_row = jnp.exp(lc_t[pl.ds(CELLS - 8, 8), :])[7:8, :]
    rel_buf[ax, pl.ds(SLOTS, 8), :] = jnp.broadcast_to(decay_row, (8, LANES))

    def send_last(offset, carry):
        pltpu.make_async_remote_copy(
            src_ref=rel_buf.at[ax], dst_ref=rel_buf.at[ax], send_sem=rel_send, recv_sem=rel_recv,
            device_id=(ax_target(offset), az), device_id_type=MESH,
        ).start()
        return carry

    def arrive(turn, last):
        c = lax.rem(turn, 2) * 2 + lax.div(turn, 2)
        own_back(c).wait()

        def add(tile, radial):
            lanes = pl.ds(tile * LANES, LANES)
            real = e_recv[c, tile, radial, 0]
            imag = e_recv[c, tile, radial, 1]
            new_real = st[radial, c, 0, :, lanes] + real + swap * (imag - real)
            new_imag = st[radial, c, 1, :, lanes] + flip * imag
            st[radial, c, 0, :, lanes] = new_real
            st[radial, c, 1, :, lanes] = new_imag
            return new_real, new_imag

        def landed(tile):
            ref = e_recv.at[c, tile, pl.ds(0, NAZ - 4)]
            pltpu.make_async_copy(ref, ref, e_recv_sem.at[0, 2 * c + tile]).wait()

            @pl.when(turn >= 2)
            def _():
                same_landed(turn, tile)

        def add_last(radial, last):
            new_real, new_imag = add(1, radial)
            where = c * 2 * NR + radial
            last = jnp.where(lane64 == where, new_real[:, LANES - 1 : LANES], last)
            return jnp.where(lane64 == where + NR, new_imag[:, LANES - 1 : LANES], last)

        def add_first(radial, carry):
            add(0, radial)
            pltpu.make_async_copy(st.at[radial, c], acc_ref.at[c, :, radial], out_sem.at[c]).start()
            return carry

        landed(1)
        last = lax.fori_loop(0, NR, add_last, last)

        @pl.when(c == FIELDS - 1)
        def _():
            rel_buf[ax, pl.ds(0, SLOTS), :] = last
            lax.fori_loop(1, NAX, send_last, 0)

        landed(0)
        lax.fori_loop(0, NR, add_first, 0)
        return last

    lax.fori_loop(0, FIELDS, arrive, jnp.zeros((SLOTS, LANES), F32))

    others = rel_buf.at[pl.ds(0, NAX - 1)]
    pltpu.make_async_copy(others, others, rel_recv).wait()

    def relay(block, incoming):
        upstream = rel_buf[block, pl.ds(0, SLOTS), :]
        decay = rel_buf[block, pl.ds(SLOTS, 8), :][0:1, :]
        return jnp.where(block < ax, decay * incoming + upstream, incoming)

    inflow = inflow_ref[...]
    inflow = jnp.concatenate([inflow, inflow], axis=1).T[:SLOTS, :]
    incoming = lax.fori_loop(0, NAX - 1, relay, inflow)
    incoming_ref[...] = jnp.concatenate([incoming, incoming], axis=0).T[:, :SLOTS]

    pltpu.make_async_copy(others, others, rel_send).wait()
    pltpu.make_async_copy(
        mode_buf.at[pl.ds(0, NAZ - 1)], mode_buf.at[pl.ds(0, NAZ - 1)], m_send
    ).wait()
    alone_sent = alone_recv.at[pl.ds(0, NAZ - 1)]
    pltpu.make_async_copy(alone_sent, alone_sent, a_send).wait()
    sent = x_buf.at[:, :, :, :, pl.ds(0, 7 * SLOTS), :]
    pltpu.make_async_copy(sent, sent, f_send).wait()
    sent_back = e_recv.at[:, :, pl.ds(0, NAZ - 1)]
    pltpu.make_async_copy(sent_back, sent_back, e_send_sem).wait()

    def written(c, carry):
        pltpu.make_async_copy(acc_ref.at[c], acc_ref.at[c], out_sem.at[c]).wait()
        return carry

    lax.fori_loop(0, FIELDS, written, 0)


def shards(state, inflow, courant, mode_number, partner_table):
    modes = mode_number.reshape(1, SLOTS)
    inflow_rows = inflow.reshape(FIELDS * 2 * NR, SLOTS)
    dma = pltpu.SemaphoreType.DMA
    vmem = pltpu.VMEM
    acc, incoming, reach = pl.pallas_call(
        kernel,
        out_shape=(
            jax.ShapeDtypeStruct((FIELDS, 2, NR, SLOTS, CELLS), F32),
            jax.ShapeDtypeStruct((FIELDS * 2 * NR, SLOTS), F32),
            jax.ShapeDtypeStruct((NR, CELLS), F32),
        ),
        in_specs=[
            pl.BlockSpec(memory_space=pl.ANY),
            pl.BlockSpec(memory_space=pltpu.VMEM),
            pl.BlockSpec(memory_space=pltpu.VMEM),
            pl.BlockSpec(memory_space=pltpu.VMEM),
        ],
        out_specs=(
            pl.BlockSpec(memory_space=pl.ANY),
            pl.BlockSpec(memory_space=pltpu.VMEM),
            pl.BlockSpec(memory_space=pltpu.VMEM),
        ),
        scratch_shapes=[
            vmem((NR, FIELDS, 2, SLOTS, CELLS), F32),
            vmem((NAZ, 2, 2, 2, 2, SLOTS, LANES), F32),
            vmem((2, 2, 2, 2, HALF, LANES), F32),
            vmem((NAZ, 8, LANES), F32),
            vmem((NAZ, 8, LANES), F32),
            vmem((2, 8, LANES), F32),
            vmem((NAZ, 8, LANES), jnp.int32),
            vmem((HALF, LANES), F32),
            vmem((SLOTS, LANES), F32),
            vmem((HALF, 3 * HALF), BF16),
            vmem((HALF, 3 * HALF), BF16),
            vmem((HALF, 3 * HALF), BF16),
            vmem((HALF, 3 * HALF), BF16),
            vmem((3 * HALF, 4 * LANES), BF16),
            vmem((3 * HALF, 4 * LANES), BF16),
            vmem((3 * CELLS, CELLS), BF16),
            vmem((2, FIELDS, HALF, LANES), F32),
            vmem((2, FIELDS, HALF, LANES), F32),
            vmem((2, FIELDS, 8, LANES), F32),
            vmem((2, 2, HALF + 8, LANES), F32),
            vmem((2, 2, HALF + 8, LANES), F32),
            vmem((NR, CELLS), F32),
            vmem((CELLS, LANES), F32),
            vmem((CELLS, LANES), F32),
            vmem((4, HALF, CELLS), F32),
            vmem((FIELDS, 2, 2, HALF, LANES), F32),
            vmem((FIELDS, 2, NAZ, 2, SLOTS, LANES), F32),
            vmem((M, 3 * CELLS), BF16),
            vmem((NAX, SLOTS + 8, LANES), F32),
            dma((NAZ,)),
            dma,
            dma((4,)),
            dma,
            dma,
            dma,
            dma,
            dma,
            dma((4,)),
            dma((4,)),
            dma,
            dma((2, 2 * FIELDS)),
            dma((FIELDS,)),
            dma((FIELDS,)),
            dma,
            dma,
        ],
        compiler_params=pltpu.CompilerParams(
            collective_id=0, has_side_effects=True, vmem_limit_bytes=58 * 2**20
        ),
    )(state, courant, modes, inflow_rows)
    incoming_full = incoming.reshape(FIELDS, 2, NR, SLOTS)
    return acc + reach[None, None, :, None, :] * incoming_full[..., None]


def solution(mesh):
    in_specs = (
        P(None, None, None, "az", "ax"),
        P(None, None, None, "az"),
        P(None, "ax"),
        P("az"),
        P("az"),
    )
    out_specs = P(None, None, None, "az", "ax")
    return jax.shard_map(shards, mesh=mesh, in_specs=in_specs, out_specs=out_specs, check_vma=False)
```

```python
import functools
import math

import jax
import jax.numpy as jnp
from jax import lax
from jax.experimental import pallas as pl
from jax.experimental.pallas import tpu as pltpu
from jax.sharding import PartitionSpec as P

section_factor = 0.5
viscosity = 0.02
M = 1024
HALF = M // 2
FIELDS = 4
NR = 16
SLOTS = 64
CELLS = 256
NAZ = 16
NAX = 8
LANES = 128
MESH = pl.DeviceIdType.MESH
F32 = jnp.float32
BF16 = jnp.bfloat16


def split(value):
    high = value.astype(BF16)
    low = (value - high.astype(F32)).astype(BF16)
    return high, low


def inverse_radius(radial_id):
    ratio = (0.6 + 0.4 * (radial_id.astype(F32) + 0.5) / NR) * (M / (2.0 * math.pi))
    return 1.0 / ratio


def cos_sin(phase):
    quadrant = lax.shift_right_logical(phase + 128, 8)
    angle = (phase - quadrant * 256).astype(F32) * (2.0 * math.pi / M)
    square = angle * angle
    sine = angle * (
        1.0
        + square
        * (-1.0 / 6 + square * (1.0 / 120 + square * (-1.0 / 5040 + square * (1.0 / 362880))))
    )
    cosine = 1.0 + square * (
        -0.5 + square * (1.0 / 24 + square * (-1.0 / 720 + square * (1.0 / 40320)))
    )
    odd = (quadrant & 1) == 1
    norm = 1.0 / math.sqrt(M)
    cos_value = jnp.where(odd, sine, cosine)
    sin_value = jnp.where(odd, cosine, sine)
    cos_sign = jnp.where(((quadrant + 1) & 2) == 2, -norm, norm)
    sin_sign = jnp.where((quadrant & 2) == 2, -norm, norm)
    return cos_value * cos_sign, sin_value * sin_sign


def signed(modes):
    return jnp.where(modes < HALF, modes, jnp.where(modes == HALF, 0.0, modes - M))


def is_self(modes):
    return jnp.where((modes == 0.0) | (modes == float(HALF)), 1.0, 0.0)


def fold_rows(value):
    rows, lanes = value.shape
    return jnp.sum(value.reshape(rows // 8, 8, lanes), axis=0)


def kernel(
    state_ref, courant_ref, mode_ref, inflow_ref,
    acc_ref, incoming_ref, reach_ref,
    st, send_buf, x_buf, alone_send, alone_recv, alone_sum, mode_buf, mode_sub, own_sub,
    cos_f, sin_f, cos_r, sin_r, rhs_a, rhs_b, tcat,
    fp, fm, fmid, halo_send, halo_recv,
    lc_ref, lc_t, om_t, e_raw, e_send, e_recv, lhs_cat, rel_buf,
    st_sem, f_send, f_recv, a_send, a_recv, m_send, m_recv, own_x, h_send, h_recv,
    e_send_sem, e_recv_sem, own_e, out_sem, rel_send, rel_recv,
):
    ax = lax.axis_index("ax")
    az = lax.axis_index("az")
    z = lax.div(az, 4)
    y = lax.rem(az, 4)

    def az_target(offset):
        step = lax.rem(offset * 7, NAZ)
        return lax.rem(z + lax.div(step, 4), 4) * 4 + lax.rem(y + lax.rem(step, 4), 4)

    def ax_target(offset):
        return lax.rem(ax + offset, NAX)

    def start_state(offset, carry):
        turn = lax.div(offset, 4)
        step = lax.rem(1 + 2 * turn + lax.div(turn, 2) * 3, 4)
        target = lax.rem(z + step, 4) * 4 + lax.rem(y + lax.rem(offset, 4), 4)
        pltpu.make_async_copy(
            state_ref.at[:, :, target], st.at[target], st_sem.at[target]
        ).start()
        return carry

    lax.fori_loop(0, NAZ, start_state, 0)

    barrier = pltpu.get_barrier_semaphore()

    def greet_az(offset, carry):
        pl.semaphore_signal(barrier, inc=1, device_id=(ax, az_target(offset)), device_id_type=MESH)
        return carry

    def greet_ax(offset, carry):
        pl.semaphore_signal(barrier, inc=1, device_id=(ax_target(offset), az), device_id_type=MESH)
        return carry

    lax.fori_loop(1, NAZ, greet_az, 0)
    lax.fori_loop(1, NAX, greet_ax, 0)

    modes_here = mode_ref[...]
    mode_buf[az] = jnp.broadcast_to(jnp.concatenate([modes_here, modes_here], axis=1), (8, LANES))

    own_sub[...] = jnp.concatenate([mode_buf[az].astype(F32)] * 16, axis=0).T[:SLOTS, :]

    group = lax.rem(z, 2) * 4 + y
    sign = jnp.where(z < 2, 1.0, -1.0)
    low_lanes = lax.broadcasted_iota(jnp.int32, (SLOTS, LANES), 1) < LANES // 2

    def column(step, dy):
        return lax.rem(z + step, 4) * 4 + lax.rem(y + dy, 4)

    def state_here(target):
        pltpu.make_async_copy(
            state_ref.at[:, :, target], st.at[target], st_sem.at[target]
        ).wait()

    def pack(step, parts):
        def body(dy, carry):
            target = column(step, dy)
            state_here(target)
            for field in range(FIELDS):
                for part in parts:
                    first = st[target, field, part, :, 0:LANES]
                    second = st[target, field, part, :, LANES:CELLS]
                    if part == 1:
                        first, second = first * sign, second * sign
                    pair, place = field % 2, field // 2
                    send_buf[target, 0, pair, place, part] = jnp.where(low_lanes, first, second)
                    send_buf[target, 1, pair, place, part] = jnp.where(low_lanes, second, first)
            return carry

        lax.fori_loop(0, 4, body, 0)

    pack(1, (0,))
    pack(3, (1,))
    pl.semaphore_wait(barrier, NAZ - 1 + NAX - 1)

    def send_modes(offset, carry):
        pltpu.make_async_remote_copy(
            src_ref=mode_buf.at[az], dst_ref=mode_buf.at[az], send_sem=m_send, recv_sem=m_recv,
            device_id=(ax, az_target(offset)), device_id_type=MESH,
        ).start()
        return carry

    lax.fori_loop(1, NAZ, send_modes, 0)

    def send_piece(chunk, pair, place, index):
        same = lax.div(index, 8)
        part = (1 - same) * lax.div(index, 4) + same * lax.rem(index, 2)
        step = (1 - same) * (1 + 2 * lax.div(index, 4))
        dy = (1 - same) * lax.rem(index, 4) + same * (lax.div(index, 2) - 3)
        target = column(step, dy)
        pltpu.make_async_remote_copy(
            src_ref=send_buf.at[target, chunk, pair, place, part],
            dst_ref=x_buf.at[chunk, pair, place, part, pl.ds(group * SLOTS, SLOTS), :],
            send_sem=f_send, recv_sem=f_recv.at[2 * pair + chunk],
            device_id=(ax, target), device_id_type=MESH,
        ).start()

    def send_first(index, carry):
        send_piece(0, 0, 0, index)
        return carry

    lax.fori_loop(0, 8, send_first, 0)
    pack(0, (0, 1))
    lax.fori_loop(8, 14, send_first, 0)

    def send_rest(piece, carry):
        def send_more(count, carry):
            send_piece(
                lax.rem(lax.div(piece, 2), 2), lax.div(piece, 4), lax.rem(piece, 2),
                lax.rem(count * 5, 14),
            )
            return carry

        return lax.fori_loop(0, 14, send_more, carry)

    lax.fori_loop(1, 2, send_rest, 0)

    own_alone = is_self(own_sub[...])

    def alone_there(dy, carry):
        state_here(column(2, dy))
        return carry

    lax.fori_loop(0, 4, alone_there, 0)

    def alone_row(radial, carry):
        rows = [[], []]
        for field in range(FIELDS):
            first = jnp.sum(own_alone * st[radial, field, 0, :, 0:LANES], axis=0, keepdims=True)
            second = jnp.sum(own_alone * st[radial, field, 0, :, LANES:CELLS], axis=0, keepdims=True)
            rows[0].append(jnp.where(low_lanes[0:1], first, second))
            rows[1].append(jnp.where(low_lanes[0:1], second, first))
        alone_send[radial] = jnp.concatenate(rows[0] + rows[1], axis=0)
        return carry

    lax.fori_loop(0, NR, alone_row, 0)
    alone_recv[az] = alone_send[az]

    def send_alone(offset, carry):
        target = az_target(offset)
        pltpu.make_async_remote_copy(
            src_ref=alone_send.at[target], dst_ref=alone_recv.at[az], send_sem=a_send,
            recv_sem=a_recv, device_id=(ax, target), device_id_type=MESH,
        ).start()
        return carry

    lax.fori_loop(1, NAZ, send_alone, 0)
    lax.fori_loop(2, 8, send_rest, 0)

    own_copy = pltpu.make_async_copy(
        send_buf.at[az], x_buf.at[:, :, :, :, pl.ds(group * SLOTS, SLOTS), :], own_x
    )
    own_copy.start()

    courant = courant_ref[...]
    weight = courant / (1.0 + courant)
    gap = 1.0 - weight
    series = gap * (
        1.0 + gap * (1.0 / 2 + gap * (1.0 / 3 + gap * (1.0 / 4 + gap * (1.0 / 5 + gap * (1.0 / 6)))))
    )
    log_weight = jnp.where(gap < 0.05, -series, jnp.log(weight))
    row_ids = lax.broadcasted_iota(jnp.int32, (CELLS, CELLS), 0)
    col_ids = lax.broadcasted_iota(jnp.int32, (CELLS, CELLS), 1)
    upper = jnp.where(row_ids <= col_ids, 1.0, 0.0)
    log_cum = jnp.dot(
        log_weight, upper, preferred_element_type=F32, precision=lax.Precision.HIGHEST
    )
    lc_ref[...] = log_cum
    reach_ref[...] = jnp.exp(log_cum)
    lc_t[...] = jnp.concatenate([log_cum] * 8, axis=0).T
    om_t[...] = jnp.concatenate([gap] * 8, axis=0).T

    def build_transfer(radial, scale):
        row = lc_ref[pl.ds(radial, 1), :]
        lanes = lax.broadcasted_iota(jnp.int32, (SLOTS, LANES), 1)

        def body(block, carry):
            rows = pl.ds(pl.multiple_of(block * SLOTS, SLOTS), SLOTS)
            pick = lanes == radial
            lc_col = jnp.sum(jnp.where(pick, lc_t[rows, :], 0.0), axis=1, keepdims=True)
            om_col = jnp.sum(jnp.where(pick, om_t[rows, :], 0.0), axis=1, keepdims=True)
            source = block * SLOTS + lax.broadcasted_iota(jnp.int32, (SLOTS, CELLS), 0)
            cell = lax.broadcasted_iota(jnp.int32, (SLOTS, CELLS), 1)
            value = jnp.where(
                source <= cell, (om_col * scale) * jnp.exp(jnp.minimum(row - lc_col, 0.0)), 0.0
            )
            high, low = split(value)
            tcat[rows, :] = high
            tcat[pl.ds(pl.multiple_of(CELLS + block * SLOTS, SLOTS), SLOTS), :] = low
            tcat[pl.ds(pl.multiple_of(2 * CELLS + block * SLOTS, SLOTS), SLOTS), :] = high
            return carry

        lax.fori_loop(0, CELLS // SLOTS, body, 0)

    build_transfer(az, section_factor)

    pltpu.make_async_copy(mode_buf.at[pl.ds(0, NAZ - 1)], mode_buf.at[pl.ds(0, NAZ - 1)], m_recv).wait()
    first_lanes = lax.broadcasted_iota(jnp.int32, (8, LANES), 1) < SLOTS
    mode_lane = [
        jnp.where(first_lanes, mode_buf[2 * q], mode_buf[2 * q + 1]) for q in range(4)
    ]
    for q in range(4):
        wide = jnp.concatenate([mode_lane[q].astype(F32)] * 16, axis=0)
        mode_sub[pl.ds(q * LANES, LANES), :] = wide.T
    mode_row = jnp.concatenate(mode_lane, axis=1)[0:1, :]

    def tables(block, carry):
        rows = pl.ds(pl.multiple_of(block * 16, 16), 16)
        point = block * 16 + lax.broadcasted_iota(jnp.int32, (16, HALF), 0)
        cos_value, sin_value = cos_sin((mode_row * point) & (M - 1))
        for table, value in ((cos_f, cos_value), (sin_f, sin_value)):
            high, low = split(value)
            table[rows, 0:HALF] = high
            table[rows, HALF : 2 * HALF] = high
            table[rows, 2 * HALF : 3 * HALF] = low
        mode_col = mode_sub[rows, :].astype(jnp.int32)
        for q in range(4):
            lane_point = q * LANES + lax.broadcasted_iota(jnp.int32, (16, LANES), 1)
            cos_value, sin_value = cos_sin((mode_col * lane_point) & (M - 1))
            cos_value = jnp.where(lane_point == 0, 0.5 * cos_value, cos_value)
            for table, value in ((cos_r, cos_value), (sin_r, sin_value)):
                high, low = split(value)
                table[rows, q * LANES : (q + 1) * LANES] = high
                table[rows, HALF + q * LANES : HALF + (q + 1) * LANES] = high
                table[rows, 2 * HALF + q * LANES : 2 * HALF + (q + 1) * LANES] = low
        return carry

    lax.fori_loop(0, HALF // 16, tables, 0)

    def self_mode(block, carry):
        modes = mode_sub[pl.ds(pl.multiple_of(block * 8, 8), 8), :]
        return carry + modes * is_self(modes)

    first_self = jnp.sum(
        lax.fori_loop(0, HALF // 8, self_mode, jnp.zeros((8, LANES), F32)), axis=0, keepdims=True
    )
    second_is_half = first_self == 0.0
    norm = 1.0 / math.sqrt(M)

    def second_cos(rows, start):
        point = start + lax.broadcasted_iota(jnp.int32, (rows, LANES), 0)
        return jnp.where(second_is_half & ((point & 1) == 1), -norm, norm)

    def put_rhs(buf, block, lanes, value):
        high, low = split(value)
        start = block * SLOTS
        buf[pl.ds(pl.multiple_of(start, SLOTS), SLOTS), lanes] = high
        buf[pl.ds(pl.multiple_of(HALF + start, SLOTS), SLOTS), lanes] = low
        buf[pl.ds(pl.multiple_of(2 * HALF + start, SLOTS), SLOTS), lanes] = high

    lane64 = lax.broadcasted_iota(jnp.int32, (SLOTS, LANES), 1)
    lane8 = lax.broadcasted_iota(jnp.int32, (8, LANES), 1)
    own_copy.wait()
    pltpu.make_async_copy(alone_send.at[pl.ds(0, NAZ - 1)], alone_recv.at[pl.ds(0, NAZ - 1)], a_recv).wait()

    def add_alone(source, total):
        return total + alone_recv[source]

    for half in range(2):
        alone_sum[half] = lax.fori_loop(
            half * (NAZ // 2), (half + 1) * (NAZ // 2), add_alone, jnp.zeros((8, LANES), F32)
        )

    def halo_copy(pair, side):
        return pltpu.make_async_remote_copy(
            src_ref=halo_send.at[pair, side], dst_ref=halo_recv.at[pair, side],
            send_sem=h_send.at[2 * pair + side], recv_sem=h_recv.at[2 * pair + side],
            device_id=(ax_target(1 if side == 0 else NAX - 1), az), device_id_type=MESH,
        )

    def send_edges(pair):
        def edges(block, carry):
            rows = pl.ds(pl.multiple_of(block * SLOTS, SLOTS), SLOTS)
            for side, lane in ((0, LANES - 1), (1, 0)):
                tile = jnp.zeros((SLOTS, LANES), F32)
                for place in range(2):
                    field = pair + 2 * place
                    tile = jnp.where(lane64 == place, fp[0, field, rows, lane : lane + 1], tile)
                    tile = jnp.where(lane64 == 4 + place, fm[0, field, rows, lane : lane + 1], tile)
                halo_send[pair, side, rows, :] = tile
            return carry

        lax.fori_loop(0, HALF // SLOTS, edges, 0)
        for side, lane in ((0, LANES - 1), (1, 0)):
            tile = jnp.zeros((8, LANES), F32)
            for place in range(2):
                tile = jnp.where(
                    lane8 == place, fmid[0, pair + 2 * place, :, lane : lane + 1], tile
                )
            halo_send[pair, side, pl.ds(HALF, 8), :] = tile
        halo_copy(pair, 0).start()
        halo_copy(pair, 1).start()

    def forward(unit, carry):
        chunk = lax.rem(unit, 2)
        pair = lax.div(unit, 2)
        arrived = x_buf.at[chunk, pair, :, :, pl.ds(0, 7 * SLOTS), :]
        pltpu.make_async_copy(arrived, arrived, f_recv.at[unit]).wait()

        def fold(block, sums):
            rows = pl.ds(pl.multiple_of(block * SLOTS, SLOTS), SLOTS)
            modes = mode_sub[rows, :]
            double = 2.0 - 2.0 * is_self(modes)
            parity = jnp.where((modes.astype(jnp.int32) & 1) == 1, -norm, norm)
            out = []
            for place in range(2):
                even = double * x_buf[chunk, pair, place, 0, rows, :]
                odd = 2.0 * x_buf[chunk, pair, place, 1, rows, :]
                put_rhs(rhs_a, block, pl.ds(place * LANES, LANES), even)
                put_rhs(rhs_b, block, pl.ds(place * LANES, LANES), odd)
                out.append(sums[place] + fold_rows(parity * even))
            return tuple(out)

        zero = jnp.zeros((8, LANES), F32)
        sums = lax.fori_loop(0, HALF // SLOTS, fold, (zero,) * 2)
        first_rows = [alone_sum[0, pl.ds(4 * chunk + pair + 2 * place, 1), :] for place in range(2)]
        second_rows = [alone_sum[1, pl.ds(4 * chunk + pair + 2 * place, 1), :] for place in range(2)]
        for place in range(2):
            middle = jnp.sum(sums[place], axis=0, keepdims=True)
            middle = middle + (first_rows[place] + second_rows[place]) * norm
            fmid[chunk, pair + 2 * place] = jnp.broadcast_to(middle, (8, LANES))
        cos_sum = jnp.dot(cos_f[...], rhs_a[:, 0:CELLS], preferred_element_type=F32)
        sin_sum = jnp.dot(sin_f[...], rhs_b[:, 0:CELLS], preferred_element_type=F32)
        for c in range(2):
            lanes = slice(c * LANES, (c + 1) * LANES)
            fp[chunk, pair + 2 * c] = cos_sum[:, lanes]
            fm[chunk, pair + 2 * c] = sin_sum[:, lanes]

        def combine(block, carry):
            rows = pl.ds(pl.multiple_of(block * SLOTS, SLOTS), SLOTS)
            point = block * SLOTS + lax.broadcasted_iota(jnp.int32, (SLOTS, LANES), 0)
            first = jnp.where((~second_is_half) & ((point & 1) == 1), -norm, norm)
            second = jnp.where(second_is_half & ((point & 1) == 1), -norm, norm)
            for c in range(2):
                even = fp[chunk, pair + 2 * c, rows, :] + first * first_rows[c]
                even = even + second * second_rows[c]
                odd = fm[chunk, pair + 2 * c, rows, :]
                fp[chunk, pair + 2 * c, rows, :] = even - odd
                fm[chunk, pair + 2 * c, rows, :] = even + odd
            return carry

        lax.fori_loop(0, HALF // SLOTS, combine, 0)

        @pl.when(chunk == 0)
        def _():
            send_edges(pair)

        return carry

    lax.fori_loop(0, 2, forward, 0)
    halo_copy(0, 0).wait()
    halo_copy(0, 1).wait()
    left_on = jnp.where(ax > 0, 1.0, 0.0)
    right_on = jnp.where(ax < NAX - 1, 1.0, 0.0)
    here = inverse_radius(az)
    here_square = here * here

    def flux_pair(get, rows, c, left_lane0, left_lanec, cell):
        def cells(field):
            outer, inner = get(0, field), get(1, field)
            low_lanes = (lane64 if rows is not None else lane8) < LANES // 2
            return jnp.concatenate(
                [jnp.where(low_lanes, outer, inner), jnp.where(low_lanes, inner, outer)], axis=1
            )

        first, this, third = cells(0), cells(c), cells(2)
        axial = first * this
        after = pltpu.roll(axial, CELLS - 1, axis=1)
        before = pltpu.roll(axial, 1, axis=1)
        left, right = left_lane0, left_lanec
        before = jnp.where(cell == 0, left, before)
        after = jnp.where(cell == CELLS - 1, right, after)
        return (before - after) * 0.5, third * this

    def pick_lane(tile, lanes, index):
        return jnp.sum(jnp.where(lanes == index, tile, 0.0), axis=1, keepdims=True)

    def own_back(c):
        return pltpu.make_async_copy(
            e_send.at[c, :, :, pl.ds(lax.rem(az, 8) * SLOTS, SLOTS), :],
            e_recv.at[c, :, az],
            own_e.at[c],
        )

    def explicit(turn, carry):
        c = lax.rem(turn, 2) * 2 + lax.div(turn, 2)

        @pl.when(turn == 2)
        def _():
            lax.fori_loop(2, 4, forward, 0)
            halo_copy(1, 0).wait()
            halo_copy(1, 1).wait()

        def fluxes(block, sums):
            rows = pl.ds(pl.multiple_of(block * SLOTS, SLOTS), SLOTS)
            cell = lax.broadcasted_iota(jnp.int32, (SLOTS, CELLS), 1)
            tile_l = halo_recv[0, 0, rows, :]
            tile_r = halo_recv[0, 1, rows, :]
            this_l = halo_recv[lax.rem(c, 2), 0, rows, :]
            this_r = halo_recv[lax.rem(c, 2), 1, rows, :]
            place = lax.div(c, 2)
            both = []
            for shift, source in ((0, fp), (4, fm)):
                left = tile_l[:, shift : shift + 1] * pick_lane(this_l, lane64, place + shift) * left_on
                right = tile_r[:, shift : shift + 1] * pick_lane(this_r, lane64, place + shift) * right_on
                both.append(
                    flux_pair(
                        lambda chunk, field, source=source: source[chunk, field, rows, :],
                        rows, c, left, right, cell,
                    )
                )
            (div_p, azi_p), (div_m, azi_m) = both
            div_even = div_p + div_m
            put_rhs(rhs_a, block, pl.ds(0, CELLS), div_even)
            put_rhs(rhs_a, block, pl.ds(CELLS, CELLS), azi_p + azi_m)
            put_rhs(rhs_b, block, pl.ds(0, CELLS), div_p - div_m)
            put_rhs(rhs_b, block, pl.ds(CELLS, CELLS), azi_p - azi_m)
            second = second_cos(SLOTS, block * SLOTS)
            point = block * SLOTS + lax.broadcasted_iota(jnp.int32, (SLOTS, LANES), 0)
            second = jnp.where(point == 0, 0.5 * second, second)
            second = jnp.concatenate([second, second], axis=1)
            return sums + fold_rows(second * div_even)

        second_sum = lax.fori_loop(0, HALF // SLOTS, fluxes, jnp.zeros((8, CELLS), F32))
        tile_l = halo_recv[0, 0, pl.ds(HALF, 8), :]
        tile_r = halo_recv[0, 1, pl.ds(HALF, 8), :]
        this_l = halo_recv[lax.rem(c, 2), 0, pl.ds(HALF, 8), :]
        this_r = halo_recv[lax.rem(c, 2), 1, pl.ds(HALF, 8), :]
        place = lax.div(c, 2)
        cell = lax.broadcasted_iota(jnp.int32, (8, CELLS), 1)
        div_mid, azi_mid = flux_pair(
            lambda chunk, field: fmid[chunk, field], None, c,
            tile_l[:, 0:1] * pick_lane(this_l, lane8, place) * left_on,
            tile_r[:, 0:1] * pick_lane(this_r, lane8, place) * right_on,
            cell,
        )
        div_mid = div_mid[0:1, :]
        azi_mid = azi_mid[0:1, :]
        second_row = jnp.sum(second_sum, axis=0, keepdims=True) + div_mid * norm

        for half in range(2):
            lanes = slice(half * CELLS, (half + 1) * CELLS)
            e_raw[half] = jnp.dot(cos_r[...], rhs_a[:, lanes], preferred_element_type=F32)
            e_raw[2 + half] = jnp.dot(sin_r[...], rhs_b[:, lanes], preferred_element_type=F32)

        def finish(block, carry):
            rows = pl.ds(pl.multiple_of(block * SLOTS, SLOTS), SLOTS)
            modes = mode_sub[rows, :]
            parity = jnp.where((modes.astype(jnp.int32) & 1) == 1, -norm, norm)
            wave = signed(modes) * here_square
            alone = is_self(modes)
            parity, wave, alone = (jnp.concatenate([v, v], axis=1) for v in (parity, wave, alone))
            cos_div = e_raw[0, rows, :] + parity * div_mid
            cos_azi = e_raw[1, rows, :] + parity * azi_mid
            real = cos_div - wave * e_raw[3, rows, :]
            imag = alone * second_row - e_raw[2, rows, :] - wave * cos_azi
            for part, value in ((0, real), (1, imag)):
                high, low = split(value)
                where = pl.ds(pl.multiple_of(part * HALF + block * SLOTS, SLOTS), SLOTS)
                lhs_cat[where, 0:CELLS] = high
                lhs_cat[where, CELLS : 2 * CELLS] = high
                lhs_cat[where, 2 * CELLS : 3 * CELLS] = low
            return carry

        lax.fori_loop(0, HALF // SLOTS, finish, 0)
        for part in range(2):
            swept = jnp.dot(
                lhs_cat[part * HALF : (part + 1) * HALF, :], tcat[...], preferred_element_type=F32
            )
            for tile in range(2):
                e_send[c, tile, part] = swept[:, tile * LANES : (tile + 1) * LANES]
        own_back(c).start()
        return carry

    def field_of(turn):
        return lax.rem(turn, 2) * 2 + lax.div(turn, 2)

    def block_back(turn, tile, part, target, same):
        c = field_of(turn)
        pltpu.make_async_remote_copy(
            src_ref=e_send.at[c, tile, part, pl.ds(lax.rem(target, 8) * SLOTS, SLOTS), :],
            dst_ref=e_recv.at[c, tile, az, part],
            send_sem=e_send_sem, recv_sem=e_recv_sem.at[same, 2 * c + tile],
            device_id=(ax, target), device_id_type=MESH,
        ).start()

    def send_back(turn, tile):
        def part_body(part, carry):
            def body(count, carry):
                index = lax.rem(count * 5, 12)
                near = lax.div(index, 8)
                same = lax.div(index, 9)
                step = (1 - near) * (1 + 2 * lax.div(index, 4)) + (near - same) * 2
                dy = (1 - near) * lax.rem(index, 4) + near * (index - 8)
                block_back(turn, tile, part, column(step, dy), same)
                return carry

            return lax.fori_loop(0, 12, body, carry)

        lax.fori_loop(0, 2, part_body, 0)

    def send_back_direct(turn, tile):
        def part_body(part, carry):
            def body(offset, carry):
                target = az_target(offset)
                step = lax.rem(lax.div(target, 4) + 4 - z, 4)
                block_back(turn, tile, part, target, 1 - lax.div(step + 3, 4))
                return carry

            return lax.fori_loop(1, NAZ, body, carry)

        lax.fori_loop(0, 2, part_body, 0)

    def same_landed(turn, tile):
        c = field_of(turn)
        ref = e_recv.at[c, tile, pl.ds(0, 3)]
        pltpu.make_async_copy(ref, ref, e_recv_sem.at[1, 2 * c + tile]).wait()

    def forward_on(turn, tile):
        c = field_of(turn)
        same_landed(turn, tile)

        def body(count, carry):
            block = e_recv.at[c, tile, column(0, 1 + lax.div(count, 2)), lax.rem(count, 2)]
            pltpu.make_async_remote_copy(
                src_ref=block, dst_ref=block,
                send_sem=e_send_sem, recv_sem=e_recv_sem.at[0, 2 * c + tile],
                device_id=(ax, column(2, 0)), device_id_type=MESH,
            ).start()
            return carry

        lax.fori_loop(0, 6, body, 0)

    def work(turn, carry):
        @pl.when(turn == 3)
        def _():
            forward_on(0, 1)
            forward_on(0, 0)

        explicit(turn, 0)

        @pl.when(turn == 3)
        def _():
            forward_on(1, 1)
            forward_on(1, 0)

        @pl.when(turn < 2)
        def _():
            send_back(turn, 1)
            send_back(turn, 0)

        @pl.when(turn == 2)
        def _():
            send_back_direct(turn, 1)
            send_back_direct(turn, 0)

        return carry

    lax.fori_loop(0, FIELDS, work, 0)
    send_back_direct(FIELDS - 1, 1)

    def state_sweep(radial, carry):
        build_transfer(radial, 1.0)
        there = inverse_radius(radial)
        ratio = signed(own_sub[...]) * there
        keep = 1.0 - (section_factor * viscosity) * ratio * ratio
        keep = jnp.concatenate([keep, keep], axis=1)
        for c in range(FIELDS):
            for part in range(2):
                high, low = split(st[radial, c, part] * keep)
                rows = pl.ds((2 * c + part) * SLOTS, SLOTS)
                lhs_cat[rows, 0:CELLS] = high
                lhs_cat[rows, CELLS : 2 * CELLS] = high
                lhs_cat[rows, 2 * CELLS : 3 * CELLS] = low
        swept = jnp.dot(lhs_cat[0:HALF, :], tcat[...], preferred_element_type=F32)
        st[radial] = swept.reshape(FIELDS, 2, SLOTS, CELLS)
        return carry

    send_back_direct(FIELDS - 1, 0)
    lax.fori_loop(0, NR, state_sweep, 0)

    low_half = jnp.where(z < 2, 1.0, 0.0)
    swap = own_alone * (1.0 - low_half)
    flip = (1.0 - own_alone) * (2.0 * low_half - 1.0)
    decay_row = jnp.exp(lc_t[pl.ds(CELLS - 8, 8), :])[7:8, :]
    rel_buf[ax, pl.ds(SLOTS, 8), :] = jnp.broadcast_to(decay_row, (8, LANES))

    def send_last(offset, carry):
        pltpu.make_async_remote_copy(
            src_ref=rel_buf.at[ax], dst_ref=rel_buf.at[ax], send_sem=rel_send, recv_sem=rel_recv,
            device_id=(ax_target(offset), az), device_id_type=MESH,
        ).start()
        return carry

    def arrive(turn, last):
        c = lax.rem(turn, 2) * 2 + lax.div(turn, 2)
        own_back(c).wait()

        def add(tile, radial):
            lanes = pl.ds(tile * LANES, LANES)
            real = e_recv[c, tile, radial, 0]
            imag = e_recv[c, tile, radial, 1]
            new_real = st[radial, c, 0, :, lanes] + real + swap * (imag - real)
            new_imag = st[radial, c, 1, :, lanes] + flip * imag
            st[radial, c, 0, :, lanes] = new_real
            st[radial, c, 1, :, lanes] = new_imag
            return new_real, new_imag

        def landed(tile):
            ref = e_recv.at[c, tile, pl.ds(0, NAZ - 4)]
            pltpu.make_async_copy(ref, ref, e_recv_sem.at[0, 2 * c + tile]).wait()

            @pl.when(turn >= 2)
            def _():
                same_landed(turn, tile)

        def add_last(radial, last):
            new_real, new_imag = add(1, radial)
            where = c * 2 * NR + radial
            last = jnp.where(lane64 == where, new_real[:, LANES - 1 : LANES], last)
            return jnp.where(lane64 == where + NR, new_imag[:, LANES - 1 : LANES], last)

        def add_first(radial, carry):
            add(0, radial)
            pltpu.make_async_copy(st.at[radial, c], acc_ref.at[c, :, radial], out_sem.at[c]).start()
            return carry

        landed(1)
        last = lax.fori_loop(0, NR, add_last, last)

        @pl.when(c == FIELDS - 1)
        def _():
            rel_buf[ax, pl.ds(0, SLOTS), :] = last
            lax.fori_loop(1, NAX, send_last, 0)

        landed(0)
        lax.fori_loop(0, NR, add_first, 0)
        return last

    lax.fori_loop(0, FIELDS, arrive, jnp.zeros((SLOTS, LANES), F32))

    others = rel_buf.at[pl.ds(0, NAX - 1)]
    pltpu.make_async_copy(others, others, rel_recv).wait()

    def relay(block, incoming):
        upstream = rel_buf[block, pl.ds(0, SLOTS), :]
        decay = rel_buf[block, pl.ds(SLOTS, 8), :][0:1, :]
        return jnp.where(block < ax, decay * incoming + upstream, incoming)

    inflow = inflow_ref[...]
    inflow = jnp.concatenate([inflow, inflow], axis=1).T[:SLOTS, :]
    incoming = lax.fori_loop(0, NAX - 1, relay, inflow)
    incoming_ref[...] = jnp.concatenate([incoming, incoming], axis=0).T[:, :SLOTS]

    pltpu.make_async_copy(others, others, rel_send).wait()
    pltpu.make_async_copy(
        mode_buf.at[pl.ds(0, NAZ - 1)], mode_buf.at[pl.ds(0, NAZ - 1)], m_send
    ).wait()
    alone_sent = alone_recv.at[pl.ds(0, NAZ - 1)]
    pltpu.make_async_copy(alone_sent, alone_sent, a_send).wait()
    sent = x_buf.at[:, :, :, :, pl.ds(0, 7 * SLOTS), :]
    pltpu.make_async_copy(sent, sent, f_send).wait()
    sent_back = e_recv.at[:, :, pl.ds(0, NAZ - 1)]
    pltpu.make_async_copy(sent_back, sent_back, e_send_sem).wait()

    def written(c, carry):
        pltpu.make_async_copy(acc_ref.at[c], acc_ref.at[c], out_sem.at[c]).wait()
        return carry

    lax.fori_loop(0, FIELDS, written, 0)


def shards(state, inflow, courant, mode_number, partner_table):
    modes = mode_number.reshape(1, SLOTS)
    inflow_rows = inflow.reshape(FIELDS * 2 * NR, SLOTS)
    dma = pltpu.SemaphoreType.DMA
    vmem = pltpu.VMEM
    acc, incoming, reach = pl.pallas_call(
        kernel,
        out_shape=(
            jax.ShapeDtypeStruct((FIELDS, 2, NR, SLOTS, CELLS), F32),
            jax.ShapeDtypeStruct((FIELDS * 2 * NR, SLOTS), F32),
            jax.ShapeDtypeStruct((NR, CELLS), F32),
        ),
        in_specs=[
            pl.BlockSpec(memory_space=pl.ANY),
            pl.BlockSpec(memory_space=pltpu.VMEM),
            pl.BlockSpec(memory_space=pltpu.VMEM),
            pl.BlockSpec(memory_space=pltpu.VMEM),
        ],
        out_specs=(
            pl.BlockSpec(memory_space=pl.ANY),
            pl.BlockSpec(memory_space=pltpu.VMEM),
            pl.BlockSpec(memory_space=pltpu.VMEM),
        ),
        scratch_shapes=[
            vmem((NR, FIELDS, 2, SLOTS, CELLS), F32),
            vmem((NAZ, 2, 2, 2, 2, SLOTS, LANES), F32),
            vmem((2, 2, 2, 2, HALF, LANES), F32),
            vmem((NAZ, 8, LANES), F32),
            vmem((NAZ, 8, LANES), F32),
            vmem((2, 8, LANES), F32),
            vmem((NAZ, 8, LANES), jnp.int32),
            vmem((HALF, LANES), F32),
            vmem((SLOTS, LANES), F32),
            vmem((HALF, 3 * HALF), BF16),
            vmem((HALF, 3 * HALF), BF16),
            vmem((HALF, 3 * HALF), BF16),
            vmem((HALF, 3 * HALF), BF16),
            vmem((3 * HALF, 4 * LANES), BF16),
            vmem((3 * HALF, 4 * LANES), BF16),
            vmem((3 * CELLS, CELLS), BF16),
            vmem((2, FIELDS, HALF, LANES), F32),
            vmem((2, FIELDS, HALF, LANES), F32),
            vmem((2, FIELDS, 8, LANES), F32),
            vmem((2, 2, HALF + 8, LANES), F32),
            vmem((2, 2, HALF + 8, LANES), F32),
            vmem((NR, CELLS), F32),
            vmem((CELLS, LANES), F32),
            vmem((CELLS, LANES), F32),
            vmem((4, HALF, CELLS), F32),
            vmem((FIELDS, 2, 2, HALF, LANES), F32),
            vmem((FIELDS, 2, NAZ, 2, SLOTS, LANES), F32),
            vmem((M, 3 * CELLS), BF16),
            vmem((NAX, SLOTS + 8, LANES), F32),
            dma((NAZ,)),
            dma,
            dma((4,)),
            dma,
            dma,
            dma,
            dma,
            dma,
            dma((4,)),
            dma((4,)),
            dma,
            dma((2, 2 * FIELDS)),
            dma((FIELDS,)),
            dma((FIELDS,)),
            dma,
            dma,
        ],
        compiler_params=pltpu.CompilerParams(
            collective_id=0, has_side_effects=True, vmem_limit_bytes=58 * 2**20
        ),
    )(state, courant, modes, inflow_rows)
    incoming_full = incoming.reshape(FIELDS, 2, NR, SLOTS)
    return acc + reach[None, None, :, None, :] * incoming_full[..., None]


def solution(mesh):
    in_specs = (
        P(None, None, None, "az", "ax"),
        P(None, None, None, "az"),
        P(None, "ax"),
        P("az"),
        P("az"),
    )
    out_specs = P(None, None, None, "az", "ax")
    return jax.shard_map(shards, mesh=mesh, in_specs=in_specs, out_specs=out_specs, check_vma=False)
```
